256 devices in a mesh: ctx: 64 (over z, x, core), dp: 4 (over y).
Axes of the slice: x: 4, y: 4, z: 8, core: 2. Of those that a mesh axis runs over, the one named last changes fastest.
Arguments:
- query_in: bfloat16 [4, 16384, 4096], P('dp', 'ctx'), may hold values from -6 to 6
- key_in: bfloat16 [4, 16384, 512], P('dp', 'ctx'), may hold values from -6 to 6
- value_rows_input: bfloat16 [4, 16384, 512], P('dp', 'ctx'), may hold values from -6 to 6
- grad_out: bfloat16 [4, 16384, 4096], P('dp', 'ctx'), may hold values from -12 to 12
- query_bias: float32 [4096], replicated, may hold values from -1.5 to 1.5
- key_blocks: int32 [4, 128, 6], P('dp'), may hold values from -1 to 127, as said below
- trace_len: int32 [4], P('dp'), may hold values from 8192 to 16384, as said below
Outputs:
- grad_query: bfloat16 [4, 16384, 4096], P('dp', 'ctx')
- grad_key: bfloat16 [4, 16384, 512], P('dp', 'ctx')
- grad_value: bfloat16 [4, 16384, 512], P('dp', 'ctx')
- bias_grad: float32 [4096], replicated
The draws below stay inside these ranges and needn't reach their ends.
Inputs may be any that keep to these rules, and one draw needn't show every extreme that they name: `key_blocks`: blocks are numbered by position. Entry 2 + d of query block q's list is q - d or -1, and entry 2 is always q; entry r < 2 is r or -1, and -1 whenever r >= q - 3. `trace_len`: some trace has 16384 tokens and some 16384 // 2.
All inputs are finite; a program needn't handle non-finite values.
Results may differ from the reference program's by a relative error of at most 0.011.
The reference program's roundings to bfloat16 on the way (of `queries`, `probs_low` and `grad_scores`) count: a program that leaves them out, or rounds other values in their place, can miss the bound.
Values may be sent and summed in bfloat16 or wider, within the bound.
A program may use at most 128 MiB of HBM per device.

```python
import math
import jax
import jax.numpy as jnp
from jax import lax

QUERY_HEADS = 32
KEY_VALUE_HEADS = 4
HEAD_SIZE = 128
BLOCK = 128
PROMPT = 2
WINDOW = 3
TRACE_COUNT = 4
NBLK = 128
TRACE_LENGTH = 16384
N_CTX = 64


def draw_query_in(key, part):
    base_value = jnp.clip(jax.random.normal(jax.random.fold_in(key, 1), (TRACE_COUNT, TRACE_LENGTH, QUERY_HEADS * HEAD_SIZE), jnp.float32), -6.0, 6.0)
    return base_value.astype(jnp.bfloat16)


def draw_key_in(key, part):
    base_value = jnp.clip(jax.random.normal(jax.random.fold_in(key, 2), (TRACE_COUNT, TRACE_LENGTH, KEY_VALUE_HEADS * HEAD_SIZE), jnp.float32), -6.0, 6.0)
    return base_value.astype(jnp.bfloat16)


def draw_grad_out(key, part):
    ramp = 1.0 + 2.0 * jnp.arange(TRACE_LENGTH, dtype=jnp.float32) / (TRACE_LENGTH - 1)
    base_value = jnp.clip(jax.random.normal(jax.random.fold_in(key, 3), (TRACE_COUNT, TRACE_LENGTH, QUERY_HEADS * HEAD_SIZE), jnp.float32), -4.0, 4.0)
    return (base_value * ramp[None, :, None]).astype(jnp.bfloat16)


def block_plan(key):
    block_idx = jnp.arange(NBLK, dtype=jnp.int32)
    starts = (jax.random.randint(jax.random.fold_in(key, 202), (TRACE_COUNT, NBLK), 0, 3, jnp.int32) == 0) & (block_idx >= PROMPT)[None]
    starts = starts | (block_idx == PROMPT)[None]
    step_id = jnp.cumsum(starts.astype(jnp.int32), axis=1)
    query_blk = block_idx[None, :, None]

    def permitted(key_blk):
        safe = jnp.clip(key_blk, 0, NBLK - 1)[0]
        key_step = jax.vmap(lambda row: row[safe])(step_id)
        query_step = step_id[:, :, None]
        nearby = (key_blk >= query_blk - WINDOW) & (key_step >= query_step - 1)
        return (key_blk >= 0) & (key_blk <= query_blk) & ((key_blk < PROMPT) | nearby)
    prompt_blk = jnp.broadcast_to(jnp.arange(PROMPT, dtype=jnp.int32)[None, None, :], (1, NBLK, PROMPT))
    window_blk = query_blk - jnp.arange(WINDOW + 1, dtype=jnp.int32)[None, None, :]
    prompt_slots = jnp.where(permitted(prompt_blk) & (prompt_blk < query_blk - WINDOW), prompt_blk, -1)
    window_slots = jnp.where(permitted(window_blk), window_blk, -1)
    return jnp.concatenate([prompt_slots, window_slots], axis=-1).astype(jnp.int32)


def draw_key_blocks(key, part):
    return block_plan(key)


def draw_trace_len(key, part):
    own_key = jax.random.fold_in(jax.random.fold_in(key, 201), part)
    lengths = jax.random.randint(jax.random.fold_in(own_key, 1), (TRACE_COUNT,), TRACE_LENGTH // 2, TRACE_LENGTH + 1, jnp.int32)
    order = jax.random.permutation(jax.random.fold_in(own_key, 2), TRACE_COUNT)
    lengths = lengths.at[order[0]].set(TRACE_LENGTH).at[order[1]].set(TRACE_LENGTH // 2)
    return lengths.astype(jnp.int32)


def shard_levels(stream_key, extent, pieces, least, high):
    factor_of, own = 1.0, jax.random.fold_in(stream_key, 6)
    for position, blocks in pieces:
        heights = jnp.exp(jax.random.uniform(jax.random.fold_in(own, position), (blocks,), jnp.float32, least / len(pieces), high / len(pieces)))
        factor_of = factor_of * jnp.repeat(heights, extent[position] // blocks).reshape([-1 if axis == position else 1 for axis in range(len(extent))])
    return factor_of


def normal_values(key, extent, deviation, limit, pieces=(), kind=jnp.bfloat16):
    entries = jax.random.normal(key, extent, jnp.float32) * deviation
    if len(pieces) > 0:
        entries = shard_levels(key, extent, pieces, -0.22, 0.18) * entries
    return jnp.clip(entries, min=-limit, max=limit).astype(kind)


def setup_inputs(seed: int = 0) -> dict:
    keys = jax.random.split(jax.random.key(seed), 8)
    query_in = draw_query_in(jax.random.fold_in(keys[7], 71), 0)
    key_in = draw_key_in(jax.random.fold_in(keys[7], 71), 0)
    value_rows_input = normal_values(keys[2], (TRACE_COUNT, TRACE_LENGTH, KEY_VALUE_HEADS * HEAD_SIZE), 1.0, 6.0, ((0, 4), (1, 64)))
    grad_out = draw_grad_out(jax.random.fold_in(keys[7], 71), 0)
    query_bias = normal_values(keys[4], (QUERY_HEADS * HEAD_SIZE,), 0.3, 1.5, (), jnp.float32)
    key_blocks = draw_key_blocks(jax.random.fold_in(keys[7], 71), 0)
    trace_len = draw_trace_len(jax.random.fold_in(keys[7], 71), 0)
    return {"query_in": query_in, "key_in": key_in, "value_rows_input": value_rows_input, "grad_out": grad_out, "query_bias": query_bias, "key_blocks": key_blocks, "trace_len": trace_len}


def unfold(stored):
    traces = stored.shape[0]
    split = stored.reshape(traces, N_CTX, 2, BLOCK, stored.shape[-1])
    return jnp.concatenate([split[:, :, 0], split[:, ::-1, 1]], axis=1)

def refold(blocks):
    traces = blocks.shape[0]
    first_half = blocks[:, :N_CTX]
    second_half = blocks[:, N_CTX:][:, ::-1]
    return jnp.stack([first_half, second_half], axis=2).reshape(traces, 2 * N_CTX * BLOCK, blocks.shape[-1])

def block_grads(queries, cand_keys, cand_vals, grad_rows, allowed):
    score_scale = HEAD_SIZE ** (-0.5)
    query_wide = queries.astype(jnp.float32)
    keys_wide = cand_keys.astype(jnp.float32)
    vals_wide = cand_vals.astype(jnp.float32)
    grad_wide = grad_rows.astype(jnp.float32)
    scores = score_scale * jnp.einsum('qkgd,skd->kgqs', query_wide, keys_wide)
    scores = jnp.where(allowed[None, None], scores, -1e+30)
    row_max = lax.optimization_barrier(jnp.max(scores, axis=-1, keepdims=True))
    probs = jnp.where(allowed[None, None], jnp.exp(scores - row_max), 0.0)
    totals = lax.optimization_barrier(jnp.sum(probs, axis=-1, keepdims=True))
    row_live = jnp.any(allowed, axis=-1)[None, None, :, None]
    probs = probs / jnp.where(row_live, totals, 1.0)
    probs_low = lax.optimization_barrier(probs.astype(jnp.bfloat16))
    probs_wide = probs_low.astype(jnp.float32)
    attended = jnp.einsum('kgqs,skd->qkgd', probs_wide, vals_wide)
    row_dot = lax.optimization_barrier(jnp.sum(grad_wide * attended, axis=-1)).transpose(1, 2, 0)[..., None]
    grad_probs = jnp.einsum('qkgd,skd->kgqs', grad_wide, vals_wide)
    grad_low = lax.optimization_barrier((probs * (grad_probs - row_dot)).astype(jnp.bfloat16))
    grad_scores = grad_low.astype(jnp.float32)
    grad_query = score_scale * jnp.einsum('kgqs,skd->qkgd', grad_scores, keys_wide)
    grad_key = score_scale * jnp.einsum('kgqs,qkgd->skd', grad_scores, query_wide)
    grad_value = jnp.einsum('kgqs,qkgd->skd', probs_wide, grad_wide)
    return (grad_query, grad_key, grad_value)

def reference(query_in, key_in, value_rows_input, grad_out, query_bias, key_blocks, trace_len):
    width_kv = key_in.shape[-1]
    width_q = query_in.shape[-1]
    heads_kv = width_kv // HEAD_SIZE
    group_size = width_q // width_kv
    cand_count = PROMPT + WINDOW + 1
    nblocks = 2 * N_CTX

    def one_trace(packed):
        query_t, key_t, value_t, grad_t, block_rows, length = packed
        queries = (query_t.astype(jnp.float32) + query_bias).astype(jnp.bfloat16)

        def visit(carry, block_idx):
            key_sum, value_sum, bias_sum = carry
            key_ids = jnp.concatenate([jnp.arange(PROMPT, dtype=jnp.int32), block_idx - jnp.arange(WINDOW + 1, dtype=jnp.int32)])
            safe_ids = jnp.clip(key_ids, 0, nblocks - 1)
            cand_keys = key_t[safe_ids].reshape(cand_count * BLOCK, heads_kv, HEAD_SIZE)
            cand_vals = value_t[safe_ids].reshape(cand_count * BLOCK, heads_kv, HEAD_SIZE)
            listed = block_rows[block_idx] >= 0
            prompt_ok = jnp.concatenate([jnp.arange(PROMPT, dtype=jnp.int32) < block_idx - WINDOW, jnp.ones((WINDOW + 1,), jnp.bool_)])
            block_ok = jnp.repeat(listed & prompt_ok, BLOCK)
            key_pos = (key_ids[:, None] * BLOCK + jnp.arange(BLOCK, dtype=jnp.int32)[None]).reshape(-1)
            query_pos = block_idx * BLOCK + jnp.arange(BLOCK, dtype=jnp.int32)
            allowed = block_ok[None] & (key_pos[None] <= query_pos[:, None]) & (key_pos[None] < length) & (query_pos[:, None] < length)
            grad_query, grad_key, grad_value = block_grads(queries[block_idx].reshape(BLOCK, heads_kv, group_size, HEAD_SIZE), cand_keys, cand_vals, grad_t[block_idx].reshape(BLOCK, heads_kv, group_size, HEAD_SIZE), allowed)
            key_sum = key_sum.at[safe_ids].add(grad_key.reshape(cand_count, BLOCK, width_kv))
            value_sum = value_sum.at[safe_ids].add(grad_value.reshape(cand_count, BLOCK, width_kv))
            flat_query = grad_query.reshape(BLOCK, width_q)
            bias_sum = bias_sum + lax.optimization_barrier(jnp.sum(flat_query, axis=0))
            return ((key_sum, value_sum, bias_sum), flat_query.astype(jnp.bfloat16))
        start = (jnp.zeros((nblocks, BLOCK, width_kv), jnp.float32), jnp.zeros((nblocks, BLOCK, width_kv), jnp.float32), jnp.zeros((width_q,), jnp.float32))
        (key_sum, value_sum, bias_sum), grad_blocks = lax.scan(visit, start, jnp.arange(nblocks, dtype=jnp.int32))
        return (grad_blocks, key_sum.astype(jnp.bfloat16), value_sum.astype(jnp.bfloat16), bias_sum)
    grad_q, grad_k, grad_v, bias_parts = lax.map(one_trace, (unfold(query_in), unfold(key_in), unfold(value_rows_input), unfold(grad_out), key_blocks, trace_len))
    bias_grad = lax.optimization_barrier(jnp.sum(bias_parts, axis=0)) / math.sqrt(TRACE_COUNT * TRACE_LENGTH)
    return (refold(grad_q), refold(grad_k), refold(grad_v), bias_grad)
```

```python
import math

import jax
import jax.numpy as jnp
from jax import lax
from jax.experimental import pallas as pl
from jax.experimental.pallas import tpu as pltpu
from jax.sharding import PartitionSpec as P

HEAD_SIZE = 128
BLOCK = 128
PROMPT = 2
WINDOW = 3
N_CTX = 64
NZ, NX, NY = 8, 4, 4
GROUPS = 4
PER_GROUP = 8
PIECE = BLOCK // NZ
SLOTS = PROMPT + WINDOW + 1
ROWS = 65536
SCALE = HEAD_SIZE ** (-0.5)
SCALE2 = SCALE * math.log2(math.e)
FAR = -1e30
BF, F32 = jnp.bfloat16, jnp.float32
MESH = pl.DeviceIdType.MESH


def dot(a, b, ca, cb):
    return lax.dot_general(a, b, (((ca,), (cb,)), ((), ())), preferred_element_type=F32)


def kernel(q_hbm, k_hbm, v_hbm, go_hbm, bias_ref, kb_ref, tl_ref,
           dq_ref, dk_ref, dv_ref, db_ref,
           qv, gv, stage, prompt, win, ret_s, ret_r, refl_r, own, pacc, ps, st1, st2s, st2,
           bsrc, b1, b2s, b2, b3s, b3,
           q_sem, g_sem, kv_sem, win_ss, win_rs, s1_ss, s1_rs, s2_ss, s2_rs, s3_ss, s3_rs,
           ret_ss, ret_rs, refl_rs, st1_ss, st1_rs, st2_ss, st2_rs, b1_ss, b1_rs, b2_ss, b2_rs, b3_ss, b3_rs):
    c = lax.axis_index("ctx")
    y = lax.axis_index("dp")
    core = lax.rem(c, 2)
    x = lax.rem(c // 2, NX)
    z = c // (2 * NX)
    gi = z * 2 + core

    def at(zz, xx, rr):
        return (zz * NX + xx) * 2 + rr

    def rcopy(src, dst, ss, rs, dev):
        return pltpu.make_async_remote_copy(src_ref=src, dst_ref=dst, send_sem=ss, recv_sem=rs,
                                            device_id={"ctx": dev}, device_id_type=MESH)

    def ycopy(src, dst, ss, rs, dev):
        return pltpu.make_async_remote_copy(src_ref=src, dst_ref=dst, send_sem=ss, recv_sem=rs,
                                            device_id={"dp": dev}, device_id_type=MESH)

    def wait_bytes(ref, sem):
        pltpu.make_async_copy(ref, ref, sem).wait()

    def loop(lo, hi, f):
        def step(i, carry):
            f(i)
            return carry
        lax.fori_loop(lo, hi, step, 0)

    def kv_load(half, kv, g):
        src = k_hbm if kv == 0 else v_hbm
        return pltpu.make_async_copy(
            src.at[pl.ds(half * BLOCK, BLOCK), pl.ds(pl.multiple_of(g * 128, 128), 128)],
            stage.at[half, g, kv], kv_sem.at[half, kv, g])

    def q_load(src, dst, sem, g):
        return pltpu.make_async_copy(
            src.at[:, pl.ds(pl.multiple_of(g * 1024, 1024), 1024)], dst.at[g], sem.at[g])

    def start_loads(g):
        for half in range(2):
            for kv in range(2):
                kv_load(half, kv, g).start()
    loop(0, GROUPS, start_loads)

    def start_q(g):
        q_load(q_hbm, qv, q_sem, g).start()
        q_load(go_hbm, gv, g_sem, g).start()
    loop(0, GROUPS, start_q)

    barrier = pltpu.get_barrier_semaphore()

    def greet(dev):
        pl.semaphore_signal(barrier, inc=1, device_id={"ctx": dev}, device_id_type=MESH)

    is_root = c < PROMPT

    def zero(g):
        refl_r[g] = jnp.zeros((WINDOW, 2, BLOCK, 128), BF)
        ret_r[1, g] = jnp.zeros((WINDOW, 2, BLOCK, 128), BF)
    loop(0, GROUPS, zero)

    for d in range(1, WINDOW + 1):
        greet(lax.rem(c + d, N_CTX))
        greet(lax.rem(c + N_CTX - d, N_CTX))

    def greet_group(k):
        j = lax.rem(gi + k, 16)
        greet(at(j // 2, x, lax.rem(j, 2)))
    loop(1, 16, greet_group)

    def greet_row(k):
        j = lax.rem(x * 2 + core + k, 8)
        greet(at(z, j // 2, lax.rem(j, 2)))
    loop(1, 8, greet_row)

    def greet_y(k):
        pl.semaphore_signal(barrier, inc=1, device_id={"dp": lax.rem(y + k, NY)}, device_id_type=MESH)
    loop(1, NY, greet_y)

    @pl.when(is_root)
    def _():
        def greet_senders(k):
            greet(k * 2 + core)
        loop(1, NZ * NX, greet_senders)

    def wait_loads(g):
        for half in range(2):
            for kv in range(2):
                kv_load(half, kv, g).wait()
    loop(0, GROUPS, wait_loads)

    @pl.when(is_root)
    def _():
        pl.semaphore_wait(barrier, 31)

    @pl.when(jnp.logical_not(is_root))
    def _():
        pl.semaphore_wait(barrier, 32)

    def piece(g, r, p):
        return prompt.at[g, r, :, pl.ds(pl.multiple_of(p * PIECE, PIECE), PIECE), :]

    @pl.when(is_root)
    def _():
        def own_piece(g):
            prompt[g, core, :, 0:PIECE, :] = stage[0, g, :, 0:PIECE, :]

            def scatter(p):
                rcopy(stage.at[0, g, :, pl.ds(pl.multiple_of(p * PIECE, PIECE), PIECE), :],
                      piece(g, core, p), s1_ss.at[g], s1_rs.at[g], at(p, 0, core)).start()
            loop(1, NZ, scatter)
        loop(0, GROUPS, own_piece)

    def win_low(g, d):
        return rcopy(stage.at[0, g], win.at[0, g, d - 1], win_ss.at[0, g, d - 1], win_rs.at[0, g, d - 1],
                     lax.rem(c + d, N_CTX))

    def win_up(g, d, half, dev):
        return rcopy(stage.at[half, g], win.at[1, g, d - 1], win_ss.at[1 + (half == 0), g, d - 1],
                     win_rs.at[1, g, d - 1], dev)

    def fold(d):
        return N_CTX * 2 - 1 - c - d

    def is_self(d):
        return c == fold(d)

    def send_window(g):
        for d in range(1, WINDOW + 1):
            win_low(g, d).start()

            @pl.when(c >= d)
            def _():
                win_up(g, d, 1, c - d).start()

            @pl.when((c >= N_CTX - d) & jnp.logical_not(is_self(d)))
            def _():
                win_up(g, d, 0, fold(d)).start()
            if d % 2 == 1:
                @pl.when(is_self(d))
                def _():
                    win[1, g, d - 1] = stage[0, g]

    def done_window(g):
        for d in range(1, WINDOW + 1):
            win_low(g, d).wait_send()

            @pl.when(c >= d)
            def _():
                win_up(g, d, 1, c - d).wait_send()

            @pl.when((c >= N_CTX - d) & jnp.logical_not(is_self(d)))
            def _():
                win_up(g, d, 0, fold(d)).wait_send()

    def wait_window(g, b):
        for d in range(1, WINDOW + 1):
            if b == 0:
                win_low(g, d).wait_recv()
            elif d % 2 == 1:
                @pl.when(jnp.logical_not(is_self(d)))
                def _():
                    win_up(g, d, 1, c).wait_recv()
            else:
                win_up(g, d, 1, c).wait_recv()

    def prompt_row(g):
        @pl.when(x == 0)
        def _():
            @pl.when(z > 0)
            def _():
                wait_bytes(piece(g, core, z), s1_rs.at[g])

            def send(k):
                j = lax.rem(core + k, 8)
                rcopy(piece(g, core, z), piece(g, core, z), s2_ss.at[g], s2_rs.at[g, core],
                      at(z, j // 2, lax.rem(j, 2))).start()
            loop(1, 8, send)

    def zpieces(g):
        return prompt.at[g, :, :, pl.ds(pl.multiple_of(z * PIECE, PIECE), PIECE), :]

    def prompt_column(g):
        for r in range(PROMPT):
            @pl.when((x > 0) | (core != r))
            def _():
                wait_bytes(piece(g, r, z), s2_rs.at[g, r])

        def send(k):
            rcopy(zpieces(g), zpieces(g), s3_ss.at[g], s3_rs.at[g], at(lax.rem(z + k, NZ), x, core)).start()
        loop(1, NZ, send)

    def seven(g):
        return prompt.at[g, :, :, pl.ds(0, (NZ - 1) * PIECE), :]

    send_window(0)
    prompt_row(0)
    prompt_row(1)
    prompt_column(0)
    loop(1, GROUPS, send_window)

    kk = lax.broadcasted_iota(jnp.int32, (BLOCK, PER_GROUP * 128), 0)
    qi = lax.rem(lax.broadcasted_iota(jnp.int32, (BLOCK, PER_GROUP * 128), 1), BLOCK)
    lane = lax.rem(lax.broadcasted_iota(jnp.int32, (1, PER_GROUP * 128), 1), BLOCK)
    length = tl_ref[0]

    def unit(g, b):
        blk = c if b == 0 else N_CTX * 2 - 1 - c
        rows = slice(b * BLOCK, (b + 1) * BLOCK)
        bias = bias_ref[pl.ds(pl.multiple_of(g * 8, 8), 8), :]
        Q = jnp.concatenate(
            [(qv[g, rows, j * 128:(j + 1) * 128].astype(F32) + bias[j:j + 1]).astype(BF) for j in range(PER_GROUP)], 0)
        G = jnp.concatenate([gv[g, rows, j * 128:(j + 1) * 128] for j in range(PER_GROUP)], 0)
        K, V = (jnp.concatenate(
            [prompt[g, 0, kv], prompt[g, 1, kv], stage[b, g, kv],
             win[b, g, 0, kv], win[b, g, 1, kv], win[b, g, 2, kv]], 0) for kv in range(2))
        off = [jnp.where(kb_ref[0, blk, s] >= 0, 0.0, FAR).astype(F32) for s in range(SLOTS)]
        S = dot(K, Q, 1, 1)
        parts, m = [], None
        for s in range(SLOTS):
            v = S[s * 128:(s + 1) * 128]
            if s == PROMPT:
                v = jnp.where(kk <= qi, v, FAR)
            parts.append(v)
            mm = jnp.max(v, 0, keepdims=True) + off[s]
            m = mm if m is None else jnp.maximum(m, mm)
        m = m * SCALE2
        exps, tot = [], None
        for s in range(SLOTS):
            p = jnp.exp2(parts[s] * SCALE2 - (m - off[s]))
            exps.append(p)
            t = jnp.sum(p, 0, keepdims=True)
            tot = t if tot is None else tot + t
        inv = jnp.where(blk * BLOCK + lane < length, 1.0 / tot, 0.0)
        probs = jnp.concatenate(exps, 0) * inv
        low = probs.astype(BF)
        dP = dot(V, G, 1, 1)
        r = jnp.sum(low.astype(F32) * dP, 0, keepdims=True)
        dS = (probs * (dP - r)).astype(BF)
        dv = dot(low, G, 1, 0)
        dk = dot(dS, Q, 1, 0) * SCALE
        dqT = dot(K, dS, 0, 0)
        for j in range(PER_GROUP):
            t = dqT[:, j * 128:(j + 1) * 128].T * SCALE
            dq_ref[rows, pl.ds(pl.multiple_of(g * 1024 + j * 128, 128), 128)] = t.astype(BF)
            t = jnp.sum(t, 0, keepdims=True)
            if b == 0:
                bsrc[g, j:j + 1, :] = t
            else:
                bsrc[g, j:j + 1, :] = bsrc[g, j:j + 1, :] + t
        for kv, val in ((0, dk), (1, dv)):
            for s in range(PROMPT):
                w = val[s * 128:(s + 1) * 128]
                if b == 0:
                    pacc[s, kv] = w
                else:
                    ps[g, s, kv] = (pacc[s, kv] + w).astype(BF)
            own[b, g, kv] = val[256:384]
            for d in range(WINDOW):
                ret_s[b, g, d, kv] = val[384 + d * 128:512 + d * 128].astype(BF)

    def ret_low(g, d):
        return rcopy(ret_s.at[0, g, d - 1], ret_r.at[0, g, d - 1], ret_ss.at[0, g, d - 1], ret_rs.at[0, g, d - 1],
                     lax.rem(c + N_CTX - d, N_CTX))

    def ret_up(g, d):
        return rcopy(ret_s.at[1, g, d - 1], ret_r.at[1, g, d - 1], ret_ss.at[1, g, d - 1], ret_rs.at[1, g, d - 1],
                     c + d)

    def ret_fold(g, d):
        return rcopy(ret_s.at[1, g, d - 1], refl_r.at[g, d - 1], ret_ss.at[1, g, d - 1], refl_rs.at[g, d - 1],
                     fold(d))

    def send_low(g):
        for d in range(1, WINDOW + 1):
            ret_low(g, d).start()

    def send_up(g):
        for d in range(1, WINDOW + 1):
            @pl.when(c + d < N_CTX)
            def _():
                ret_up(g, d).start()

            @pl.when((c + d >= N_CTX) & jnp.logical_not(is_self(d)))
            def _():
                ret_fold(g, d).start()
            if d % 2 == 1:
                @pl.when(is_self(d))
                def _():
                    refl_r[g, d - 1] = ret_s[1, g, d - 1]

    def done_ret(g):
        for d in range(1, WINDOW + 1):
            ret_low(g, d).wait_send()
            @pl.when(jnp.logical_not(is_self(d)))
            def _():
                ret_up(g, d).wait_send()

    def wait_ret(g):
        for d in range(1, WINDOW + 1):
            ret_low(g, d).wait_recv()

            @pl.when(c >= d)
            def _():
                ret_up(g, d).wait_recv()

            @pl.when((c >= N_CTX - d) & jnp.logical_not(is_self(d)))
            def _():
                ret_fold(g, d).wait_recv()

    def send_shared(g):
        def send(k):
            j = lax.rem(gi + k, 16)
            zj, rj = j // 2, lax.rem(j, 2)
            dev = at(zj, x, rj)
            rcopy(ps.at[g, rj, :, pl.ds(pl.multiple_of(zj * PIECE, PIECE), PIECE), :], st1.at[g, gi],
                  st1_ss.at[g], st1_rs.at[g], dev).start()
            rcopy(bsrc.at[g], b1.at[g, gi], b1_ss.at[g], b1_rs.at[g], dev).start()
        loop(1, 16, send)

    def step1(g):
        st1[g, gi] = ps[g, core, :, pl.ds(pl.multiple_of(z * PIECE, PIECE), PIECE), :]
        b1[g, gi] = bsrc[g]
        wait_bytes(b1.at[g, pl.ds(0, 15)], b1_rs.at[g])
        total = b1[g, 0]
        for k in range(1, 16):
            total = total + b1[g, k]
        b2s[g] = total
        b2[g, x] = total

        def send(k):
            rcopy(b2s.at[g], b2.at[g, x], b2_ss.at[g], b2_rs.at[g], at(z, lax.rem(x + k, NX), core)).start()
        loop(1, NX, send)
        wait_bytes(st1.at[g, pl.ds(0, 15)], st1_rs.at[g])
        total = st1[g, 0].astype(F32)
        for k in range(1, 16):
            total = total + st1[g, k].astype(F32)
        st2s[g] = total.astype(BF)

        @pl.when(is_root)
        def _():
            st2[g, 0] = st2s[g]

        @pl.when(jnp.logical_not(is_root))
        def _():
            rcopy(st2s.at[g], st2.at[g, z * NX + x], st2_ss.at[g], st2_rs.at[g], core).start()

    def step2(g):
        wait_bytes(b2.at[g, pl.ds(0, NX - 1)], b2_rs.at[g])
        total = b2[g, 0]
        for k in range(1, NX):
            total = total + b2[g, k]
        b3s[g] = total
        b3[g, y] = total

        def send(k):
            ycopy(b3s.at[g], b3.at[g, y], b3_ss.at[g], b3_rs.at[g], lax.rem(y + k, NY)).start()
        loop(1, NY, send)

    def step3(g):
        wait_bytes(b3.at[g, pl.ds(0, NY - 1)], b3_rs.at[g])
        total = b3[g, 0]
        for k in range(1, NY):
            total = total + b3[g, k]
        db_ref[pl.ds(pl.multiple_of(g * 8, 8), 8), :] = total * (1.0 / math.sqrt(ROWS))

    def finish(g):
        wait_ret(g)
        cols = pl.ds(pl.multiple_of(g * 128, 128), 128)
        for kv, out in ((0, dk_ref), (1, dv_ref)):
            first, second = own[0, g, kv], own[1, g, kv]
            for d in range(WINDOW):
                first = first + ret_r[0, g, d, kv].astype(F32) + refl_r[g, d, kv].astype(F32)
                second = second + ret_r[1, g, d, kv].astype(F32)
            own[0, g, kv] = first
            out[0:BLOCK, cols] = first.astype(BF)
            out[BLOCK:2 * BLOCK, cols] = second.astype(BF)

    def finish_root(g):
        wait_bytes(st2.at[g, pl.ds(0, NZ * NX - 1)], st2_rs.at[g])
        cols = pl.ds(pl.multiple_of(g * 128, 128), 128)
        for kv, out in ((0, dk_ref), (1, dv_ref)):
            for p in range(NZ):
                rr = slice(p * PIECE, (p + 1) * PIECE)
                total = own[0, g, kv, rr, :]
                for k in range(NX):
                    total = total + st2[g, p * NX + k, kv].astype(F32)
                out[rr, cols] = total.astype(BF)

    def main(g):
        q_load(q_hbm, qv, q_sem, g).wait()
        q_load(go_hbm, gv, g_sem, g).wait()
        wait_bytes(seven(g), s3_rs.at[g])
        wait_window(g, 0)
        unit(g, 0)
        send_low(g)

        @pl.when(g + 2 < GROUPS)
        def _():
            prompt_row(g + 2)

        @pl.when(g + 1 < GROUPS)
        def _():
            prompt_column(g + 1)

        @pl.when(g > 0)
        def _():
            step1(g - 1)
        wait_window(g, 1)
        unit(g, 1)
        send_shared(g)
        send_up(g)

        @pl.when(g > 0)
        def _():
            step2(g - 1)
    loop(0, GROUPS, main)

    last = GROUPS - 1
    loop(0, last, finish)
    step1(last)
    finish(last)
    step2(last)

    @pl.when(is_root)
    def _():
        loop(0, GROUPS, finish_root)
    loop(0, GROUPS, step3)

    def drain(g):
        done_window(g)
        done_ret(g)

        @pl.when(is_root)
        def _():
            wait_bytes(prompt.at[g, 0, :, pl.ds(0, (NZ - 1) * PIECE), :], s1_ss.at[g])

        @pl.when(jnp.logical_not(is_root))
        def _():
            wait_bytes(st2s.at[g], st2_ss.at[g])

        @pl.when(x == 0)
        def _():
            wait_bytes(prompt.at[g, 0, :, pl.ds(0, 7 * PIECE), :], s2_ss.at[g])
        wait_bytes(seven(g), s3_ss.at[g])
        wait_bytes(st1.at[g, pl.ds(0, 15)], st1_ss.at[g])
        wait_bytes(b1.at[g, pl.ds(0, 15)], b1_ss.at[g])
        wait_bytes(b2.at[g, pl.ds(0, NX - 1)], b2_ss.at[g])
        wait_bytes(b3.at[g, pl.ds(0, NY - 1)], b3_ss.at[g])
    loop(0, GROUPS, drain)


def body(query_in, key_in, value_rows_input, grad_out, query_bias, key_blocks, trace_len):
    any_ = pl.BlockSpec(memory_space=pl.ANY)
    vmem = pl.BlockSpec(memory_space=pltpu.VMEM)
    smem = pl.BlockSpec(memory_space=pltpu.SMEM)
    dma = pltpu.SemaphoreType.DMA
    tile = (2, BLOCK, 128)
    G = GROUPS
    dq, dk, dv, db = pl.pallas_call(
        kernel,
        out_shape=(
            jax.ShapeDtypeStruct((2 * BLOCK, 4096), BF),
            jax.ShapeDtypeStruct((2 * BLOCK, 512), BF),
            jax.ShapeDtypeStruct((2 * BLOCK, 512), BF),
            jax.ShapeDtypeStruct((32, 128), F32),
        ),
        in_specs=[any_, any_, any_, any_, vmem, smem, smem],
        out_specs=(vmem, vmem, vmem, vmem),
        scratch_shapes=[
            pltpu.VMEM((G, 2 * BLOCK, 1024), BF),
            pltpu.VMEM((G, 2 * BLOCK, 1024), BF),
            pltpu.VMEM((2, G) + tile, BF),
            pltpu.VMEM((G, PROMPT) + tile, BF),
            pltpu.VMEM((2, G, WINDOW) + tile, BF),
            pltpu.VMEM((2, G, WINDOW) + tile, BF),
            pltpu.VMEM((2, G, WINDOW) + tile, BF),
            pltpu.VMEM((G, WINDOW) + tile, BF),
            pltpu.VMEM((2, G) + tile, F32),
            pltpu.VMEM((PROMPT,) + tile, F32),
            pltpu.VMEM((G, PROMPT) + tile, BF),
            pltpu.VMEM((G, 16, 2, PIECE, 128), BF),
            pltpu.VMEM((G, 2, PIECE, 128), BF),
            pltpu.VMEM((G, NZ * NX, 2, PIECE, 128), BF),
            pltpu.VMEM((G, 8, 128), F32),
            pltpu.VMEM((G, 16, 8, 128), F32),
            pltpu.VMEM((G, 8, 128), F32),
            pltpu.VMEM((G, NX, 8, 128), F32),
            pltpu.VMEM((G, 8, 128), F32),
            pltpu.VMEM((G, NY, 8, 128), F32),
            dma((G,)), dma((G,)), dma((2, 2, G)),
            dma((3, G, WINDOW)), dma((2, G, WINDOW)),
            dma((G,)), dma((G,)), dma((G,)), dma((G, PROMPT)), dma((G,)), dma((G,)),
            dma((2, G, WINDOW)), dma((2, G, WINDOW)), dma((G, WINDOW)),
            dma((G,)), dma((G,)), dma((G,)), dma((G,)),
            dma((G,)), dma((G,)), dma((G,)), dma((G,)), dma((G,)), dma((G,)),
        ],
        compiler_params=pltpu.CompilerParams(
            collective_id=0, has_side_effects=True, vmem_limit_bytes=58 * 2**20),
        name="attention",
    )(query_in[0], key_in[0], value_rows_input[0], grad_out[0], query_bias.reshape(32, 128), key_blocks, trace_len)
    return dq[None], dk[None], dv[None], db.reshape(4096)


def solution(mesh):
    return jax.shard_map(
        body,
        mesh=mesh,
        in_specs=(
            P("dp", "ctx", None),
            P("dp", "ctx", None),
            P("dp", "ctx", None),
            P("dp", "ctx", None),
            P(),
            P("dp", None, None),
            P("dp"),
        ),
        out_specs=(P("dp", "ctx", None), P("dp", "ctx", None), P("dp", "ctx", None), P()),
        check_vma=False,
    )
```

```python
import math

import jax
import jax.numpy as jnp
from jax import lax
from jax.experimental import pallas as pl
from jax.experimental.pallas import tpu as pltpu
from jax.sharding import PartitionSpec as P

HEAD_SIZE = 128
BLOCK = 128
PROMPT = 2
WINDOW = 3
NBLK = 128
N_CTX = 64
CHIPS = 32
NZ, NX, NY = 8, 4, 4
GROUPS = 2
PER_GROUP = 8
PIECE = BLOCK // NZ
SLOTS = PROMPT + WINDOW + 1
NEAR = 5
ROWS = 65536
SCALE = HEAD_SIZE ** (-0.5)
SCALE2 = SCALE * math.log2(math.e)
FAR = -1e30
BF, F32 = jnp.bfloat16, jnp.float32
MESH = pl.DeviceIdType.MESH


def dot(a, b, ca, cb):
    return lax.dot_general(a, b, (((ca,), (cb,)), ((), ())), preferred_element_type=F32)


def kernel(q_hbm, k_hbm, v_hbm, go_hbm, bias_ref, kb_ref, tl_ref,
           dq_ref, dk_ref, dv_ref, db_ref,
           qv, gv, stage, prompt, cand, acc, pacc, dqs, ret_s, ret_r, refl_r, sib_s, sib_r,
           ps, st1, st2s, st2, st3s, st3, bsrc, b1, b2s, b2, b3s, b3,
           q_sem, g_sem, kv_sem, own_sem, qx_ss, qx_rs, gx_ss, gx_rs, cx_ss, cx_rs,
           win_ss, win_rs, s1_ss, s1_rs, s2_ss, s2_rs, s3_ss, s3_rs, dq_ss, dq_rs,
           ret_ss, ret_rs, refl_rs, sib_ss, sib_rs, st1_ss, st1_rs, st2_ss, st2_rs, st3_ss, st3_rs,
           b1_ss, b1_rs, b2_ss, b2_rs, b3_ss, b3_rs):
    c = lax.axis_index("ctx")
    y = lax.axis_index("dp")
    core = lax.rem(c, 2)
    other = 1 - core
    chip = c // 2
    x = lax.rem(chip, NX)
    z = chip // NX
    sibling = chip * 2 + other
    is_root = c < PROMPT

    def at(zz, xx, rr):
        return (zz * NX + xx) * 2 + rr

    def rcopy(src, dst, ss, rs, dev):
        return pltpu.make_async_remote_copy(src_ref=src, dst_ref=dst, send_sem=ss, recv_sem=rs,
                                            device_id={"ctx": dev}, device_id_type=MESH)

    def wait_bytes(ref, sem):
        pltpu.make_async_copy(ref, ref, sem).wait()

    def loop(lo, hi, f):
        def step(i, carry):
            f(i)
            return carry
        lax.fori_loop(lo, hi, step, 0)

    def span(start, size):
        return pl.ds(pl.multiple_of(start, size), size)

    def kv_copy(half, kv, head, dst, sem):
        src = k_hbm if kv == 0 else v_hbm
        return pltpu.make_async_copy(src.at[half * BLOCK:(half + 1) * BLOCK, span(head * 128, 128)], dst, sem)

    def mine(half):
        return other if half == 0 else core

    def kv_stage(half, kv, head):
        return kv_copy(half, kv, head, stage.at[half, head, kv], kv_sem.at[half, kv, head])

    def kv_own(half, kv, g):
        return kv_copy(half, kv, core * 2 + g, cand.at[half, g, mine(half), kv], own_sem.at[half, kv, g])

    def q_own(src, dst, sem, g):
        return pltpu.make_async_copy(src.at[:, span(core * 2048 + g * 1024, 1024)], dst.at[1, g], sem.at[g])

    def q_cross(src, dst, ss, rs, g):
        return rcopy(src.at[:, span(other * 2048 + g * 1024, 1024)], dst.at[0, g], ss.at[g], rs.at[g], sibling)

    def start_stage(h):
        for half in range(2):
            for kv in range(2):
                kv_stage(half, kv, h).start()
    loop(0, 4, start_stage)

    def start_own(g):
        for half in range(2):
            for kv in range(2):
                kv_own(half, kv, g).start()
        q_own(q_hbm, qv, q_sem, g).start()
        q_own(go_hbm, gv, g_sem, g).start()
    loop(0, GROUPS, start_own)

    barrier = pltpu.get_barrier_semaphore()

    def greet(dev, yy):
        pl.semaphore_signal(barrier, inc=1, device_id={"ctx": dev, "dp": yy}, device_id_type=MESH)

    def greet_near(k):
        away = lax.rem(chip + CHIPS - 2 + k, CHIPS)

        @pl.when(k != 2)
        def _():
            greet(away * 2, y)
            greet(away * 2 + 1, y)
    loop(0, 5, greet_near)

    gi = z * 2 + core

    def greet_group(k):
        j = lax.rem(gi + k, 16)
        greet(at(j // 2, x, lax.rem(j, 2)), y)
    loop(1, 16, greet_group)

    def greet_row(k):
        greet(at(z, lax.rem(x + k, NX), core), y)
    loop(1, NX, greet_row)

    def greet_y(k):
        yy = lax.rem(y + k, NY)
        greet(c, yy)
        greet(sibling, yy)
    loop(1, NY, greet_y)

    def zero(g):
        for half in range(2):
            ret_r[half, g] = jnp.zeros((2, 2, 2, BLOCK, 128), BF)
            acc[half, g] = jnp.zeros((NEAR, 2, BLOCK, 128), F32)
        refl_r[g] = jnp.zeros((2, 2, BLOCK, 128), BF)
        pacc[g] = jnp.zeros((PROMPT, 2, BLOCK, 128), F32)
        bsrc[g] = jnp.zeros((8, 128), F32)
    loop(0, GROUPS, zero)

    def wait_stage(h):
        for half in range(2):
            for kv in range(2):
                kv_stage(half, kv, h).wait()
    loop(0, 4, wait_stage)

    pl.semaphore_wait(barrier, 8 + 15 + 3 + 6)

    def rows16(p):
        return span(p * PIECE, PIECE)

    @pl.when(is_root)
    def _():
        def scatter_group(g):
            prompt[g, c, :, 0:PIECE, :] = stage[0, c * 2 + g, :, 0:PIECE, :]

            def scatter(k):
                j = lax.rem(c + k, 16)
                p, r = j // 2, lax.rem(j, 2)
                rcopy(stage.at[0, r * 2 + g, :, rows16(p), :], prompt.at[g, c, :, rows16(p), :],
                      s1_ss.at[g], s1_rs.at[g, c], at(p, 0, r)).start()
            loop(1, 16, scatter)
        loop(0, GROUPS, scatter_group)

    def win_low(g, r, far):
        dst = lax.rem(chip + 1 + far, CHIPS) * 2 + r
        slot = 4 if far else 1 + 2 - core
        return rcopy(stage.at[0, r * 2 + g], cand.at[0, g, slot], win_ss.at[0, g, r, far], win_rs.at[0, g, slot - 2], dst)

    def win_up(g, r, far):
        dst = (chip - 1 - far) * 2 + r
        slot = 4 if far else 1 + 1 + core
        return rcopy(stage.at[1, r * 2 + g], cand.at[1, g, slot], win_ss.at[1, g, r, far], win_rs.at[1, g, slot - 2], dst)

    def win_fold(g, r):
        return rcopy(stage.at[0, r * 2 + g], cand.at[1, g, 4], win_ss.at[1, g, r, 1], win_rs.at[1, g, 2],
                     N_CTX - 4 + r)

    def cross(half, g):
        slot = mine(half)
        return rcopy(stage.at[half, other * 2 + g], cand.at[half, g, slot], cx_ss.at[half, g], cx_rs.at[half, g], sibling)

    def each_window(g, act):
        for r in range(2):
            act(win_low(g, r, 0))

            @pl.when(chip >= 1)
            def _():
                act(win_up(g, r, 0))

            @pl.when(core == 1)
            def _():
                act(win_low(g, r, 1))

            @pl.when((core == 0) & (chip >= 2))
            def _():
                act(win_up(g, r, 1))

            @pl.when(c == N_CTX - 1)
            def _():
                act(win_fold(g, r))
        for half in range(2):
            act(cross(half, g))
        act(q_cross(q_hbm, qv, qx_ss, qx_rs, g))
        act(q_cross(go_hbm, gv, gx_ss, gx_rs, g))

    def wait_near(g, half):
        cross(half, g).wait_recv()
        for slot in range(2, NEAR):
            rcopy(cand.at[half, g, slot], cand.at[half, g, slot], win_ss.at[0, g, 0, 0], win_rs.at[half, g, slot - 2],
                  sibling).wait_recv()

    def prompt_piece(g):
        return prompt.at[g, :, :, rows16(z), :]

    def prompt_row(g):
        @pl.when(x == 0)
        def _():
            for r in range(PROMPT):
                @pl.when(c != r)
                def _():
                    wait_bytes(prompt.at[g, r, :, rows16(z), :], s1_rs.at[g, r])

            def send(k):
                rcopy(prompt_piece(g), prompt_piece(g), s2_ss.at[g], s2_rs.at[g], at(z, k, core)).start()
            loop(1, NX, send)

    def prompt_column(g):
        @pl.when(x > 0)
        def _():
            wait_bytes(prompt_piece(g), s2_rs.at[g])

        def send(k):
            rcopy(prompt_piece(g), prompt_piece(g), s3_ss.at[g], s3_rs.at[g], at(lax.rem(z + k, NZ), x, core)).start()
        loop(1, NZ, send)

    def pieces(ref, g, n):
        return ref.at[g, :, :, pl.ds(0, n * PIECE), :]

    each_window(0, lambda copy: copy.start())
    prompt_row(0)
    prompt_column(0)
    each_window(1, lambda copy: copy.start())
    prompt_row(1)

    width = PER_GROUP * 128
    kk = lax.broadcasted_iota(jnp.int32, (BLOCK, width), 0)
    qi = lax.rem(lax.broadcasted_iota(jnp.int32, (BLOCK, width), 1), BLOCK)
    lane = lax.rem(lax.broadcasted_iota(jnp.int32, (1, width), 1), BLOCK)
    length = tl_ref[0]

    def unit(g, half, role):
        rho = core if role else other
        dev = chip * 2 + rho
        blk = jnp.where(half == 0, dev, NBLK - 1 - dev)
        base = jnp.where(half == 0, 1 - rho, rho)
        rows = span(half * BLOCK, BLOCK)
        bias = bias_ref[span(core * 16 + g * 8, 8), :]
        Q = jnp.concatenate(
            [(qv[role, g, rows, j * 128:(j + 1) * 128].astype(F32) + bias[j:j + 1]).astype(BF)
             for j in range(PER_GROUP)], 0)
        G = jnp.concatenate([gv[role, g, rows, j * 128:(j + 1) * 128] for j in range(PER_GROUP)], 0)
        K, V = (jnp.concatenate(
            [prompt[g, s, kv] for s in range(PROMPT)] + [cand[half, g, base + d, kv] for d in range(WINDOW + 1)], 0)
            for kv in range(2))
        off = [jnp.where(kb_ref[s * NBLK + blk] >= 0, 0.0, FAR).astype(F32) for s in range(SLOTS)]
        S = dot(K, Q, 1, 1)
        parts, m = [], None
        for s in range(SLOTS):
            v = S[s * 128:(s + 1) * 128]
            if s == PROMPT:
                v = jnp.where(kk <= qi, v, FAR)
            parts.append(v)
            mm = jnp.max(v, 0, keepdims=True) + off[s]
            m = mm if m is None else jnp.maximum(m, mm)
        m = m * SCALE2
        exps, tot = [], None
        for s in range(SLOTS):
            p = jnp.exp2(parts[s] * SCALE2 - (m - off[s]))
            exps.append(p)
            t = jnp.sum(p, 0, keepdims=True)
            tot = t if tot is None else tot + t
        inv = jnp.where(blk * BLOCK + lane < length, 1.0 / tot, 0.0)
        probs = jnp.concatenate(exps, 0) * inv
        low = probs.astype(BF)
        dP = dot(V, G, 1, 1)
        r = jnp.sum(low.astype(F32) * dP, 0, keepdims=True)
        dS = (probs * (dP - r)).astype(BF)
        dv = dot(low, G, 1, 0)
        dk = dot(dS, Q, 1, 0) * SCALE
        dqT = dot(K, dS, 0, 0)
        for j in range(PER_GROUP):
            t = dqT[:, j * 128:(j + 1) * 128].T * SCALE
            if role:
                dq_ref[rows, span(core * 2048 + g * 1024 + j * 128, 128)] = t.astype(BF)
            else:
                dqs[g, rows, j * 128:(j + 1) * 128] = t.astype(BF)
            bsrc[g, j:j + 1, :] = bsrc[g, j:j + 1, :] + jnp.sum(t, 0, keepdims=True)
        for kv, val in ((0, dk), (1, dv)):
            for s in range(PROMPT):
                pacc[g, s, kv] = pacc[g, s, kv] + val[s * 128:(s + 1) * 128]
            for d in range(WINDOW + 1):
                acc[half, g, base + d, kv] = acc[half, g, base + d, kv] + val[256 + d * 128:384 + d * 128]

    def dq_cross(g, half):
        rows = span(half * BLOCK, BLOCK)
        return rcopy(dqs.at[g, rows, :], dq_ref.at[rows, span(core * 2048 + g * 1024, 1024)],
                     dq_ss.at[g, half], dq_rs.at[g, half], sibling)

    def ret_low(g, e):
        far = 1 if e == 3 else 0
        return rcopy(ret_s.at[0, g, e - 1], ret_r.at[0, g, core, far], ret_ss.at[0, g, e - 1],
                     ret_rs.at[0, g, core, far], lax.rem(chip * 2 + N_CTX - e, N_CTX))

    def ret_up(g, e):
        far = 1 if e == 3 else 0
        return rcopy(ret_s.at[1, g, e - 1], ret_r.at[1, g, core, far], ret_ss.at[1, g, e - 1],
                     ret_rs.at[1, g, core, far], chip * 2 + 1 + e)

    def ret_fold(g):
        return rcopy(ret_s.at[1, g, 2], refl_r.at[g, core], ret_ss.at[1, g, 2], refl_rs.at[g, core], N_CTX - 1)

    def sib_copy(g, half):
        return rcopy(sib_s.at[half, g], sib_r.at[half, g], sib_ss.at[half, g], sib_rs.at[half, g], sibling)

    def each_low(g, act):
        for e in range(1, WINDOW + 1):
            act(ret_low(g, e))
        act(sib_copy(g, 0))

    def each_up(g, act):
        for e in range(1, WINDOW + 1):
            @pl.when(chip * 2 + 1 + e < N_CTX)
            def _():
                act(ret_up(g, e))

        @pl.when(chip == CHIPS - 2)
        def _():
            act(ret_fold(g))
        act(sib_copy(g, 1))

    def send_low(g):
        for e in range(WINDOW):
            ret_s[0, g, e] = acc[0, g, 2 + e].astype(BF)
        sib_s[0, g] = acc[0, g, core].astype(BF)
        each_low(g, lambda copy: copy.start())

    def send_up(g):
        for e in range(WINDOW):
            ret_s[1, g, e] = acc[1, g, 2 + e].astype(BF)
        sib_s[1, g] = acc[1, g, other].astype(BF)
        each_up(g, lambda copy: copy.start())

    def fold_sums(g):
        for e in range(WINDOW):
            acc[0, g, e] = acc[0, g, e] + acc[1, g, 2 + e]

    def wait_recv(ref, sem):
        rcopy(ref, ref, win_ss.at[0, 0, 0, 0], sem, sibling).wait_recv()

    def wait_ret(g):
        for r in range(2):
            wait_recv(ret_r.at[0, g, r, 0], ret_rs.at[0, g, r, 0])

            @pl.when(core == 1)
            def _():
                wait_recv(ret_r.at[0, g, r, 1], ret_rs.at[0, g, r, 1])

            @pl.when(chip >= 1)
            def _():
                wait_recv(ret_r.at[1, g, r, 0], ret_rs.at[1, g, r, 0])

            @pl.when((core == 0) & (chip >= 2))
            def _():
                wait_recv(ret_r.at[1, g, r, 1], ret_rs.at[1, g, r, 1])

            @pl.when(c == N_CTX - 1)
            def _():
                wait_recv(refl_r.at[g, r], refl_rs.at[g, r])
        for half in range(2):
            wait_recv(sib_r.at[half, g], sib_rs.at[half, g])

    def send_shared(g):
        ps[g] = pacc[g].astype(BF)

        def send(k):
            zj = lax.rem(z + k, NZ)
            dev = at(zj, x, core)
            rcopy(ps.at[g, :, :, rows16(zj), :], st1.at[g, z], st1_ss.at[g], st1_rs.at[g], dev).start()
            rcopy(bsrc.at[g], b1.at[g, z], b1_ss.at[g], b1_rs.at[g], dev).start()
        loop(1, NZ, send)
        st1[g, z] = ps[g, :, :, rows16(z), :]
        b1[g, z] = bsrc[g]

    def total_of(ref, g, n):
        total = ref[g, 0].astype(F32)
        for k in range(1, n):
            total = total + ref[g, k].astype(F32)
        return total

    def step1(g):
        wait_bytes(st1.at[g, pl.ds(0, NZ - 1)], st1_rs.at[g])
        st2s[g] = total_of(st1, g, NZ).astype(BF)

        @pl.when(x == 0)
        def _():
            st2[g, 0] = st2s[g]

        @pl.when(x > 0)
        def _():
            rcopy(st2s.at[g], st2.at[g, x], st2_ss.at[g], st2_rs.at[g], at(z, 0, core)).start()
        wait_bytes(b1.at[g, pl.ds(0, NZ - 1)], b1_rs.at[g])
        total = total_of(b1, g, NZ)
        b2s[g] = total
        b2[g, x] = total

        def send(k):
            rcopy(b2s.at[g], b2.at[g, x], b2_ss.at[g], b2_rs.at[g], at(z, lax.rem(x + k, NX), core)).start()
        loop(1, NX, send)

    def to_root(g, root):
        return rcopy(st3s.at[g, root], st3.at[g, core * NZ + z], st3_ss.at[g, root], st3_rs.at[g], root)

    def step2(g):
        @pl.when(x == 0)
        def _():
            wait_bytes(st2.at[g, pl.ds(0, NX - 1)], st2_rs.at[g])
            st3s[g] = total_of(st2, g, NX).astype(BF)
            for root in range(PROMPT):
                @pl.when(c == root)
                def _():
                    st3[g, root * NZ] = st3s[g, root]

                @pl.when(c != root)
                def _():
                    to_root(g, root).start()
        wait_bytes(b2.at[g, pl.ds(0, NX - 1)], b2_rs.at[g])
        total = total_of(b2, g, NX)
        b3s[g] = total
        b3[g, core * NY + y] = total

        def send(k):
            j = lax.rem(core * NY + y + k, 2 * NY)
            pltpu.make_async_remote_copy(
                src_ref=b3s.at[g], dst_ref=b3.at[g, core * NY + y], send_sem=b3_ss.at[g], recv_sem=b3_rs.at[g],
                device_id={"ctx": chip * 2 + j // NY, "dp": lax.rem(j, NY)}, device_id_type=MESH).start()
        loop(1, 2 * NY, send)

    def step3(g):
        wait_bytes(b3.at[g, pl.ds(0, 2 * NY - 1)], b3_rs.at[g])
        for r in range(2):
            total = b3[g, r * NY]
            for k in range(1, NY):
                total = total + b3[g, r * NY + k]
            db_ref[span(r * 16 + g * 8, 8), :] = total * (1.0 / math.sqrt(ROWS))

    def finish(g):
        wait_ret(g)
        for t in range(2):
            r = other if t else core
            cols = span((r * 2 + g) * 128, 128)
            for half in range(2):
                for kv, out in ((0, dk_ref), (1, dv_ref)):
                    total = sib_r[half, g, kv].astype(F32) if t else acc[half, g, mine(half), kv]
                    for far in range(2):
                        total = total + ret_r[half, g, r, far, kv].astype(F32)
                    if half == 0:
                        total = total + refl_r[g, r, kv].astype(F32)

                        @pl.when(is_root)
                        def _():
                            pacc[g, t, kv] = total
                    out[half * BLOCK:(half + 1) * BLOCK, cols] = total.astype(BF)

    def finish_root(g):
        wait_bytes(st3.at[g, pl.ds(0, 2 * NZ - 1)], st3_rs.at[g])
        for t in range(2):
            r = other if t else core
            cols = span((r * 2 + g) * 128, 128)
            for kv, out in ((0, dk_ref), (1, dv_ref)):
                for p in range(NZ):
                    rr = slice(p * PIECE, (p + 1) * PIECE)
                    out[rr, cols] = (pacc[g, t, kv, rr, :] + st3[g, r * NZ + p, kv].astype(F32)).astype(BF)

    def main(i):
        g, half = i // 2, lax.rem(i, 2)

        @pl.when(half == 0)
        def _():
            for kv in range(2):
                kv_own(0, kv, g).wait()
                kv_own(1, kv, g).wait()
            q_own(q_hbm, qv, q_sem, g).wait()
            q_own(go_hbm, gv, g_sem, g).wait()
            q_cross(q_hbm, qv, qx_ss, qx_rs, g).wait_recv()
            q_cross(go_hbm, gv, gx_ss, gx_rs, g).wait_recv()
            wait_near(g, 0)
            wait_bytes(pieces(prompt, g, NZ - 1), s3_rs.at[g])

        @pl.when(half == 1)
        def _():
            cross(1, g).wait_recv()

            @pl.when(chip < CHIPS - 1)
            def _():
                for slot in range(2, NEAR):
                    wait_recv(cand.at[1, g, slot], win_rs.at[1, g, slot - 2])

            @pl.when(chip == CHIPS - 1)
            def _():
                for slot in range(2, NEAR):
                    cand[1, g, slot] = cand[0, g, slot - 2]
        unit(g, half, 0)
        dq_cross(g, half).start()

        @pl.when(i == 0)
        def _():
            prompt_column(1)

        @pl.when(i == 2)
        def _():
            step1(0)
        unit(g, half, 1)

        @pl.when(half == 1)
        def _():
            send_shared(g)

            @pl.when(chip == CHIPS - 1)
            def _():
                fold_sums(g)
                send_low(g)
            send_up(g)

        @pl.when((half == 0) & (chip < CHIPS - 1))
        def _():
            send_low(g)

        @pl.when(i == 2)
        def _():
            step2(0)
    loop(0, 2 * GROUPS, main)

    finish(0)
    step1(1)
    finish(1)
    step2(1)
    step3(0)

    @pl.when(is_root)
    def _():
        loop(0, GROUPS, finish_root)
    step3(1)

    def drain(g):
        for half in range(2):
            dq_cross(g, half).wait()
        each_window(g, lambda copy: copy.wait_send())
        each_low(g, lambda copy: copy.wait_send())
        each_up(g, lambda copy: copy.wait_send())

        @pl.when(is_root)
        def _():
            wait_bytes(st3.at[g, pl.ds(0, 2 * NZ - 1)], s1_ss.at[g])

        @pl.when(x == 0)
        def _():
            wait_bytes(pieces(prompt, g, NX - 1), s2_ss.at[g])
            for root in range(PROMPT):
                @pl.when(c != root)
                def _():
                    to_root(g, root).wait_send()

        @pl.when(x > 0)
        def _():
            wait_bytes(st2s.at[g], st2_ss.at[g])
        wait_bytes(pieces(prompt, g, NZ - 1), s3_ss.at[g])
        wait_bytes(st1.at[g, pl.ds(0, NZ - 1)], st1_ss.at[g])
        wait_bytes(b1.at[g, pl.ds(0, NZ - 1)], b1_ss.at[g])
        wait_bytes(b2.at[g, pl.ds(0, NX - 1)], b2_ss.at[g])
        wait_bytes(b3.at[g, pl.ds(0, 2 * NY - 1)], b3_ss.at[g])
    loop(0, GROUPS, drain)


def body(query_in, key_in, value_rows_input, grad_out, query_bias, key_blocks, trace_len):
    any_ = pl.BlockSpec(memory_space=pl.ANY)
    vmem = pl.BlockSpec(memory_space=pltpu.VMEM)
    smem = pl.BlockSpec(memory_space=pltpu.SMEM)
    dma = pltpu.SemaphoreType.DMA
    tile = (2, BLOCK, 128)
    G = GROUPS

    def many(*dims):
        return pltpu.VMEM(dims + tile, BF)
    part = (PROMPT, 2, PIECE, 128)
    dq, dk, dv, db = pl.pallas_call(
        kernel,
        out_shape=(
            pltpu.VMEM((2 * BLOCK, 4096), BF),
            pltpu.VMEM((2 * BLOCK, 512), BF),
            pltpu.VMEM((2 * BLOCK, 512), BF),
            pltpu.VMEM((32, 128), F32),
        ),
        in_specs=[any_, any_, any_, any_, vmem, smem, smem],
        out_specs=(vmem, vmem, vmem, vmem),
        scratch_shapes=[
            pltpu.VMEM((2, G, 2 * BLOCK, 1024), BF), pltpu.VMEM((2, G, 2 * BLOCK, 1024), BF),
            many(2, 4), many(G, PROMPT), many(2, G, NEAR),
            pltpu.VMEM((2, G, NEAR) + tile, F32), pltpu.VMEM((G, PROMPT) + tile, F32),
            pltpu.VMEM((G, 2 * BLOCK, 1024), BF),
            many(2, G, WINDOW), many(2, G, 2, 2), many(G, 2), many(2, G), many(2, G),
            many(G, PROMPT),
            pltpu.VMEM((G, NZ) + part, BF), pltpu.VMEM((G,) + part, BF), pltpu.VMEM((G, NX) + part, BF),
            pltpu.VMEM((G,) + part, BF), pltpu.VMEM((G, 2 * NZ, 2, PIECE, 128), BF),
            pltpu.VMEM((G, 8, 128), F32), pltpu.VMEM((G, NZ, 8, 128), F32),
            pltpu.VMEM((G, 8, 128), F32), pltpu.VMEM((G, NX, 8, 128), F32),
            pltpu.VMEM((G, 8, 128), F32), pltpu.VMEM((G, 2 * NY, 8, 128), F32),
            dma((G,)), dma((G,)), dma((2, 2, 4)), dma((2, 2, G)),
            dma((G,)), dma((G,)), dma((G,)), dma((G,)), dma((2, G)), dma((2, G)),
            dma((2, G, 2, 2)), dma((2, G, WINDOW)),
            dma((G,)), dma((G, PROMPT)), dma((G,)), dma((G,)), dma((G,)), dma((G,)), dma((G, 2)), dma((G, 2)),
            dma((2, G, WINDOW)), dma((2, G, 2, 2)), dma((G, 2)), dma((2, G)), dma((2, G)),
            dma((G,)), dma((G,)), dma((G,)), dma((G,)), dma((G, PROMPT)), dma((G,)),
            dma((G,)), dma((G,)), dma((G,)), dma((G,)), dma((G,)), dma((G,)),
        ],
        compiler_params=pltpu.CompilerParams(
            collective_id=0, has_side_effects=True, vmem_limit_bytes=58 * 2**20),
        name="attention",
    )(query_in[0], key_in[0], value_rows_input[0], grad_out[0], query_bias.reshape(32, 128),
      key_blocks.transpose(2, 0, 1).reshape(-1), trace_len)
    return dq[None], dk[None], dv[None], db.reshape(4096)


def solution(mesh):
    return jax.shard_map(
        body,
        mesh=mesh,
        in_specs=(
            P("dp", "ctx", None),
            P("dp", "ctx", None),
            P("dp", "ctx", None),
            P("dp", "ctx", None),
            P(),
            P("dp", None, None),
            P("dp"),
        ),
        out_specs=(P("dp", "ctx", None), P("dp", "ctx", None), P("dp", "ctx", None), P()),
        check_vma=False,
    )
```

```python
import math

import jax
import jax.numpy as jnp
from jax import lax
from jax.experimental import pallas as pl
from jax.experimental.pallas import tpu as pltpu
from jax.sharding import PartitionSpec as P

HEAD_SIZE = 128
BLOCK = 128
PROMPT = 2
WINDOW = 3
NBLK = 128
N_CTX = 64
CHIPS = 32
NZ, NX, NY = 8, 4, 4
GROUPS = 2
PER_GROUP = 8
PIECE = BLOCK // NZ
SLOTS = PROMPT + WINDOW + 1
NEAR = 5
ROWS = 65536
SCALE = HEAD_SIZE ** (-0.5)
SCALE2 = SCALE * math.log2(math.e)
FAR = -1e30
BF, F32 = jnp.bfloat16, jnp.float32
MESH = pl.DeviceIdType.MESH


def dot(a, b, ca, cb):
    return lax.dot_general(a, b, (((ca,), (cb,)), ((), ())), preferred_element_type=F32)


def kernel(q_hbm, k_hbm, v_hbm, go_hbm, bias_ref, kb_ref, tl_ref,
           dq_ref, dk_ref, dv_ref, db_ref,
           qv, gv, stage, prompt, cand, acc, pacc, dqs, ret_s, ret_r, refl_r, sib_s, sib_r,
           ps, st1, st2s, st2, st3s, st3, bsrc, b1, b2s, b2, b3s, b3,
           q_sem, g_sem, kv_sem, own_sem, qx_ss, qx_rs, gx_ss, gx_rs, cx_ss, cx_rs,
           win_ss, win_rs, s1_ss, s1_rs, s2_ss, s2_rs, s3_ss, s3_rs, dq_ss, dq_rs,
           ret_ss, ret_rs, refl_rs, sib_ss, sib_rs, st1_ss, st1_rs, st2_ss, st2_rs, st3_ss, st3_rs,
           b1_ss, b1_rs, b2_ss, b2_rs, b3_ss, b3_rs):
    c = lax.axis_index("ctx")
    y = lax.axis_index("dp")
    core = lax.rem(c, 2)
    other = 1 - core
    chip = c // 2
    x = lax.rem(chip, NX)
    z = chip // NX
    sibling = chip * 2 + other
    is_root = c < PROMPT

    def at(zz, xx, rr):
        return (zz * NX + xx) * 2 + rr

    def rcopy(src, dst, ss, rs, dev):
        return pltpu.make_async_remote_copy(src_ref=src, dst_ref=dst, send_sem=ss, recv_sem=rs,
                                            device_id={"ctx": dev}, device_id_type=MESH)

    def wait_bytes(ref, sem):
        pltpu.make_async_copy(ref, ref, sem).wait()

    def loop(lo, hi, f):
        def step(i, carry):
            f(i)
            return carry
        lax.fori_loop(lo, hi, step, 0)

    def span(start, size):
        return pl.ds(pl.multiple_of(start, size), size)

    def kv_copy(half, kv, head, dst, sem):
        src = k_hbm if kv == 0 else v_hbm
        return pltpu.make_async_copy(src.at[half * BLOCK:(half + 1) * BLOCK, span(head * 128, 128)], dst, sem)

    def mine(half):
        return other if half == 0 else core

    def kv_stage(half, kv, head):
        return kv_copy(half, kv, head, stage.at[half, head, kv], kv_sem.at[half, kv, head])

    def kv_own(half, kv, g):
        return kv_copy(half, kv, core * 2 + g, cand.at[half, g, mine(half), kv], own_sem.at[half, kv, g])

    def q_own(src, dst, sem, g):
        return pltpu.make_async_copy(src.at[:, span(core * 2048 + g * 1024, 1024)], dst.at[1, g], sem.at[g])

    def q_cross(src, dst, ss, rs, g):
        return rcopy(src.at[:, span(other * 2048 + g * 1024, 1024)], dst.at[0, g], ss.at[g], rs.at[g], sibling)

    def start_stage(h):
        for half in range(2):
            for kv in range(2):
                kv_stage(half, kv, h).start()
    loop(0, 4, start_stage)

    def start_own(g):
        for half in range(2):
            for kv in range(2):
                kv_own(half, kv, g).start()
        q_own(q_hbm, qv, q_sem, g).start()
        q_own(go_hbm, gv, g_sem, g).start()
    loop(0, GROUPS, start_own)

    barrier = pltpu.get_barrier_semaphore()

    def greet(dev, yy):
        pl.semaphore_signal(barrier, inc=1, device_id={"ctx": dev, "dp": yy}, device_id_type=MESH)

    def greet_near(k):
        away = lax.rem(chip + CHIPS - 2 + k, CHIPS)

        @pl.when(k != 2)
        def _():
            greet(away * 2, y)
            greet(away * 2 + 1, y)
    loop(0, 5, greet_near)

    gi = z * 2 + core

    def greet_group(k):
        j = lax.rem(gi + k, 16)
        greet(at(j // 2, x, lax.rem(j, 2)), y)
    loop(1, 16, greet_group)

    def greet_row(k):
        greet(at(z, lax.rem(x + k, NX), core), y)
    loop(1, NX, greet_row)

    def greet_y(k):
        yy = lax.rem(y + k, NY)
        greet(c, yy)
        greet(sibling, yy)
    loop(1, NY, greet_y)

    def zero(g):
        for half in range(2):
            ret_r[half, g] = jnp.zeros((2, 2, 2, BLOCK, 128), BF)
            acc[half, g] = jnp.zeros((NEAR, 2, BLOCK, 128), F32)
        refl_r[g] = jnp.zeros((2, 2, BLOCK, 128), BF)
        pacc[g] = jnp.zeros((PROMPT, 2, BLOCK, 128), F32)
        bsrc[g] = jnp.zeros((8, 128), F32)
    loop(0, GROUPS, zero)

    def wait_stage(h):
        for half in range(2):
            for kv in range(2):
                kv_stage(half, kv, h).wait()
    loop(0, 4, wait_stage)

    pl.semaphore_wait(barrier, 8 + 15 + 3 + 6)

    def rows16(p):
        return span(p * PIECE, PIECE)

    def scatter_prompt(g):
        @pl.when(is_root)
        def _():
            prompt[g, c, :, 0:PIECE, :] = stage[0, c * 2 + g, :, 0:PIECE, :]

            def scatter(k):
                j = lax.rem(c + k, 16)
                p, r = j // 2, lax.rem(j, 2)
                rcopy(stage.at[0, r * 2 + g, :, rows16(p), :], prompt.at[g, c, :, rows16(p), :],
                      s1_ss.at[g], s1_rs.at[g, c], at(p, 0, r)).start()
            loop(1, 16, scatter)
    scatter_prompt(0)

    def win_low(g, r, far):
        dst = lax.rem(chip + 1 + far, CHIPS) * 2 + r
        slot = 4 if far else 1 + 2 - core
        return rcopy(stage.at[0, r * 2 + g], cand.at[0, g, slot], win_ss.at[0, g, r, far], win_rs.at[0, g, slot - 2], dst)

    def win_up(g, r, far):
        dst = (chip - 1 - far) * 2 + r
        slot = 4 if far else 1 + 1 + core
        return rcopy(stage.at[1, r * 2 + g], cand.at[1, g, slot], win_ss.at[1, g, r, far], win_rs.at[1, g, slot - 2], dst)

    def win_fold(g, r):
        return rcopy(stage.at[0, r * 2 + g], cand.at[1, g, 4], win_ss.at[1, g, r, 1], win_rs.at[1, g, 2],
                     N_CTX - 4 + r)

    def cross(half, g):
        slot = mine(half)
        return rcopy(stage.at[half, other * 2 + g], cand.at[half, g, slot], cx_ss.at[half, g], cx_rs.at[half, g], sibling)

    def each_window(g, act):
        for r in range(2):
            act(win_low(g, r, 0))

            @pl.when(chip >= 1)
            def _():
                act(win_up(g, r, 0))

            @pl.when(core == 1)
            def _():
                act(win_low(g, r, 1))

            @pl.when((core == 0) & (chip >= 2))
            def _():
                act(win_up(g, r, 1))

            @pl.when(c == N_CTX - 1)
            def _():
                act(win_fold(g, r))
        for half in range(2):
            act(cross(half, g))
        act(q_cross(q_hbm, qv, qx_ss, qx_rs, g))
        act(q_cross(go_hbm, gv, gx_ss, gx_rs, g))

    def wait_near(g, half):
        cross(half, g).wait_recv()
        for slot in range(2, NEAR):
            rcopy(cand.at[half, g, slot], cand.at[half, g, slot], win_ss.at[0, g, 0, 0], win_rs.at[half, g, slot - 2],
                  sibling).wait_recv()

    def prompt_piece(g):
        return prompt.at[g, :, :, rows16(z), :]

    def prompt_row(g):
        @pl.when(x == 0)
        def _():
            for r in range(PROMPT):
                @pl.when(c != r)
                def _():
                    wait_bytes(prompt.at[g, r, :, rows16(z), :], s1_rs.at[g, r])

            def send(k):
                rcopy(prompt_piece(g), prompt_piece(g), s2_ss.at[g], s2_rs.at[g], at(z, k, core)).start()
            loop(1, NX, send)

    def prompt_column(g):
        @pl.when(x > 0)
        def _():
            wait_bytes(prompt_piece(g), s2_rs.at[g])

        def send(k):
            rcopy(prompt_piece(g), prompt_piece(g), s3_ss.at[g], s3_rs.at[g], at(lax.rem(z + k, NZ), x, core)).start()
        loop(1, NZ, send)

    def pieces(ref, g, n):
        return ref.at[g, :, :, pl.ds(0, n * PIECE), :]

    each_window(0, lambda copy: copy.start())
    prompt_row(0)
    prompt_column(0)

    width = PER_GROUP * 128
    kk = lax.broadcasted_iota(jnp.int32, (BLOCK, width), 0)
    qi = lax.rem(lax.broadcasted_iota(jnp.int32, (BLOCK, width), 1), BLOCK)
    lane = lax.rem(lax.broadcasted_iota(jnp.int32, (1, width), 1), BLOCK)
    length = tl_ref[0]

    def unit(g, half, role, leave=None):
        rho = core if role else other
        dev = chip * 2 + rho
        blk = jnp.where(half == 0, dev, NBLK - 1 - dev)
        base = jnp.where(half == 0, 1 - rho, rho)
        rows = span(half * BLOCK, BLOCK)
        bias = bias_ref[span(core * 16 + g * 8, 8), :]
        Q = jnp.concatenate(
            [(qv[role, g, rows, j * 128:(j + 1) * 128].astype(F32) + bias[j:j + 1]).astype(BF)
             for j in range(PER_GROUP)], 0)
        G = jnp.concatenate([gv[role, g, rows, j * 128:(j + 1) * 128] for j in range(PER_GROUP)], 0)
        K, V = (jnp.concatenate(
            [prompt[g, s, kv] for s in range(PROMPT)] + [cand[half, g, base + d, kv] for d in range(WINDOW + 1)], 0)
            for kv in range(2))
        off = [jnp.where(kb_ref[s, 0, blk] >= 0, 0.0, FAR).astype(F32) for s in range(SLOTS)]
        S = dot(K, Q, 1, 1)
        parts, m = [], None
        for s in range(SLOTS):
            v = S[s * 128:(s + 1) * 128]
            if s == PROMPT:
                v = jnp.where(kk <= qi, v, FAR)
            parts.append(v)
            mm = jnp.max(v, 0, keepdims=True) + off[s]
            m = mm if m is None else jnp.maximum(m, mm)
        m = m * SCALE2
        exps, tot = [], None
        for s in range(SLOTS):
            p = jnp.exp2(parts[s] * SCALE2 - (m - off[s]))
            exps.append(p)
            t = jnp.sum(p, 0, keepdims=True)
            tot = t if tot is None else tot + t
        inv = jnp.where(blk * BLOCK + lane < length, 1.0 / tot, 0.0)
        probs = jnp.concatenate(exps, 0) * inv
        low = probs.astype(BF)
        dP = dot(V, G, 1, 1)
        r = jnp.sum(probs * dP, 0, keepdims=True)
        dS = (probs * (dP - r)).astype(BF)
        dv = dot(low, G, 1, 0)
        dk = dot(dS, Q, 1, 0) * SCALE
        for kv, val in ((0, dk), (1, dv)):
            for s in range(PROMPT):
                pacc[g, s, kv] = pacc[g, s, kv] + val[s * 128:(s + 1) * 128]
            for d in range(WINDOW + 1):
                acc[half, g, base + d, kv] = acc[half, g, base + d, kv] + val[256 + d * 128:384 + d * 128]
        if leave is not None:
            leave()
        dq = dot(dS, K, 0, 0)
        for j in range(PER_GROUP):
            t = dq[j * 128:(j + 1) * 128] * SCALE
            if role:
                dq_ref[rows, span(core * 2048 + g * 1024 + j * 128, 128)] = t.astype(BF)
            else:
                dqs[g, rows, j * 128:(j + 1) * 128] = t.astype(BF)
            bsrc[g, j:j + 1, :] = bsrc[g, j:j + 1, :] + jnp.sum(t, 0, keepdims=True)

    def dq_cross(g, half):
        rows = span(half * BLOCK, BLOCK)
        return rcopy(dqs.at[g, rows, :], dq_ref.at[rows, span(core * 2048 + g * 1024, 1024)],
                     dq_ss.at[g, half], dq_rs.at[g, half], sibling)

    def ret_low(g, e):
        far = 1 if e == 3 else 0
        return rcopy(ret_s.at[0, g, e - 1], ret_r.at[0, g, core, far], ret_ss.at[0, g, e - 1],
                     ret_rs.at[0, g, core, far], lax.rem(chip * 2 + N_CTX - e, N_CTX))

    def ret_up(g, e):
        far = 1 if e == 3 else 0
        return rcopy(ret_s.at[1, g, e - 1], ret_r.at[1, g, core, far], ret_ss.at[1, g, e - 1],
                     ret_rs.at[1, g, core, far], chip * 2 + 1 + e)

    def ret_fold(g):
        return rcopy(ret_s.at[1, g, 2], refl_r.at[g, core], ret_ss.at[1, g, 2], refl_rs.at[g, core], N_CTX - 1)

    def sib_copy(g, half):
        return rcopy(sib_s.at[half, g], sib_r.at[half, g], sib_ss.at[half, g], sib_rs.at[half, g], sibling)

    def each_low(g, act):
        for e in range(1, WINDOW + 1):
            act(ret_low(g, e))
        act(sib_copy(g, 0))

    def each_up(g, act):
        for e in range(1, WINDOW + 1):
            @pl.when(chip * 2 + 1 + e < N_CTX)
            def _():
                act(ret_up(g, e))

        @pl.when(chip == CHIPS - 2)
        def _():
            act(ret_fold(g))
        act(sib_copy(g, 1))

    def send_low(g):
        for e in range(WINDOW):
            ret_s[0, g, e] = acc[0, g, 2 + e].astype(BF)
        sib_s[0, g] = acc[0, g, core].astype(BF)
        each_low(g, lambda copy: copy.start())

    def send_up(g):
        for e in range(WINDOW):
            ret_s[1, g, e] = acc[1, g, 2 + e].astype(BF)
        sib_s[1, g] = acc[1, g, other].astype(BF)
        each_up(g, lambda copy: copy.start())

    def fold_sums(g):
        for e in range(WINDOW):
            acc[0, g, e] = acc[0, g, e] + acc[1, g, 2 + e]

    def wait_recv(ref, sem):
        rcopy(ref, ref, win_ss.at[0, 0, 0, 0], sem, sibling).wait_recv()

    def wait_ret(g):
        for r in range(2):
            wait_recv(ret_r.at[0, g, r, 0], ret_rs.at[0, g, r, 0])

            @pl.when(core == 1)
            def _():
                wait_recv(ret_r.at[0, g, r, 1], ret_rs.at[0, g, r, 1])

            @pl.when(chip >= 1)
            def _():
                wait_recv(ret_r.at[1, g, r, 0], ret_rs.at[1, g, r, 0])

            @pl.when((core == 0) & (chip >= 2))
            def _():
                wait_recv(ret_r.at[1, g, r, 1], ret_rs.at[1, g, r, 1])

            @pl.when(c == N_CTX - 1)
            def _():
                wait_recv(refl_r.at[g, r], refl_rs.at[g, r])
        for half in range(2):
            wait_recv(sib_r.at[half, g], sib_rs.at[half, g])

    def send_shared(g):
        ps[g] = pacc[g].astype(BF)

        def send(k):
            zj = lax.rem(z + k, NZ)
            dev = at(zj, x, core)
            rcopy(ps.at[g, :, :, rows16(zj), :], st1.at[g, z], st1_ss.at[g], st1_rs.at[g], dev).start()
        loop(1, NZ, send)
        st1[g, z] = ps[g, :, :, rows16(z), :]

    def total_of(ref, g, n):
        total = ref[g, 0].astype(F32)
        for k in range(1, n):
            total = total + ref[g, k].astype(F32)
        return total

    def step1(g):
        wait_bytes(st1.at[g, pl.ds(0, NZ - 1)], st1_rs.at[g])
        st2s[g] = total_of(st1, g, NZ).astype(BF)

        @pl.when(x == 0)
        def _():
            st2[g, 0] = st2s[g]

        @pl.when(x > 0)
        def _():
            rcopy(st2s.at[g], st2.at[g, x], st2_ss.at[g], st2_rs.at[g], at(z, 0, core)).start()
    def to_root(g, root):
        return rcopy(st3s.at[g, root], st3.at[g, core * NZ + z], st3_ss.at[g, root], st3_rs.at[g], root)

    def step2(g):
        @pl.when(x == 0)
        def _():
            wait_bytes(st2.at[g, pl.ds(0, NX - 1)], st2_rs.at[g])
            st3s[g] = total_of(st2, g, NX).astype(BF)
            for root in range(PROMPT):
                @pl.when(c == root)
                def _():
                    st3[g, root * NZ] = st3s[g, root]

                @pl.when(c != root)
                def _():
                    to_root(g, root).start()
    def send_bias():
        def send(k):
            rcopy(bsrc, b1.at[z], b1_ss, b1_rs, at(lax.rem(z + k, NZ), x, core)).start()
        loop(1, NZ, send)
        b1[z] = bsrc[...]

    def sum_bias(ref, n):
        total = ref[0]
        for k in range(1, n):
            total = total + ref[k]
        return total

    def bias1():
        wait_bytes(b1.at[pl.ds(0, NZ - 1)], b1_rs)
        total = sum_bias(b1, NZ)
        b2s[...] = total
        b2[x] = total

        def send(k):
            rcopy(b2s, b2.at[x], b2_ss, b2_rs, at(z, lax.rem(x + k, NX), core)).start()
        loop(1, NX, send)

    def bias2():
        wait_bytes(b2.at[pl.ds(0, NX - 1)], b2_rs)
        total = sum_bias(b2, NX)
        b3s[...] = total
        b3[core * NY + y] = total

        def send(k):
            j = lax.rem(core * NY + y + k, 2 * NY)
            pltpu.make_async_remote_copy(
                src_ref=b3s, dst_ref=b3.at[core * NY + y], send_sem=b3_ss, recv_sem=b3_rs,
                device_id={"ctx": chip * 2 + j // NY, "dp": lax.rem(j, NY)}, device_id_type=MESH).start()
        loop(1, 2 * NY, send)

    def bias3():
        wait_bytes(b3.at[pl.ds(0, 2 * NY - 1)], b3_rs)
        for r in range(2):
            total = b3[r * NY]
            for k in range(1, NY):
                total = total + b3[r * NY + k]
            for g in range(GROUPS):
                db_ref[r * 16 + g * 8:r * 16 + g * 8 + 8, :] = total[g] * (1.0 / math.sqrt(ROWS))

    def finish(g):
        wait_ret(g)
        for t in range(2):
            r = other if t else core
            cols = span((r * 2 + g) * 128, 128)
            for half in range(2):
                for kv, out in ((0, dk_ref), (1, dv_ref)):
                    total = sib_r[half, g, kv].astype(F32) if t else acc[half, g, mine(half), kv]
                    for far in range(2):
                        total = total + ret_r[half, g, r, far, kv].astype(F32)
                    if half == 0:
                        total = total + refl_r[g, r, kv].astype(F32)

                        @pl.when(is_root)
                        def _():
                            pacc[g, t, kv] = total
                    out[half * BLOCK:(half + 1) * BLOCK, cols] = total.astype(BF)

    def finish_root(g):
        wait_bytes(st3.at[g, pl.ds(0, 2 * NZ - 1)], st3_rs.at[g])
        for t in range(2):
            r = other if t else core
            cols = span((r * 2 + g) * 128, 128)
            for kv, out in ((0, dk_ref), (1, dv_ref)):
                for p in range(NZ):
                    rr = slice(p * PIECE, (p + 1) * PIECE)
                    out[rr, cols] = (pacc[g, t, kv, rr, :] + st3[g, r * NZ + p, kv].astype(F32)).astype(BF)

    def main(i):
        g, half = i // 2, lax.rem(i, 2)

        @pl.when(half == 0)
        def _():
            for kv in range(2):
                kv_own(0, kv, g).wait()
                kv_own(1, kv, g).wait()
            q_own(q_hbm, qv, q_sem, g).wait()
            q_own(go_hbm, gv, g_sem, g).wait()
            q_cross(q_hbm, qv, qx_ss, qx_rs, g).wait_recv()
            q_cross(go_hbm, gv, gx_ss, gx_rs, g).wait_recv()
            wait_near(g, 0)
            wait_bytes(pieces(prompt, g, NZ - 1), s3_rs.at[g])

        @pl.when(i == 0)
        def _():
            scatter_prompt(1)
            each_window(1, lambda copy: copy.start())

        @pl.when(half == 1)
        def _():
            cross(1, g).wait_recv()

            @pl.when(chip < CHIPS - 1)
            def _():
                for slot in range(2, NEAR):
                    wait_recv(cand.at[1, g, slot], win_rs.at[1, g, slot - 2])

            @pl.when(chip == CHIPS - 1)
            def _():
                for slot in range(2, NEAR):
                    cand[1, g, slot] = cand[0, g, slot - 2]
        unit(g, half, 0)
        dq_cross(g, half).start()

        @pl.when(i == 0)
        def _():
            prompt_row(1)

        @pl.when(i == 2)
        def _():
            step1(0)

        def leave():
            @pl.when(half == 1)
            def _():
                send_shared(g)

                @pl.when(chip == CHIPS - 1)
                def _():
                    fold_sums(g)
                    send_low(g)
                send_up(g)

            @pl.when((half == 0) & (chip < CHIPS - 1))
            def _():
                send_low(g)
        unit(g, half, 1, leave)

        @pl.when(i == 0)
        def _():
            prompt_column(1)

        @pl.when(i == 2)
        def _():
            step2(0)
    loop(0, 2 * GROUPS, main)

    def drain(g):
        for half in range(2):
            dq_cross(g, half).wait()
        each_window(g, lambda copy: copy.wait_send())
        each_low(g, lambda copy: copy.wait_send())
        each_up(g, lambda copy: copy.wait_send())

        @pl.when(is_root)
        def _():
            wait_bytes(st3.at[g, pl.ds(0, 2 * NZ - 1)], s1_ss.at[g])

        @pl.when(x == 0)
        def _():
            wait_bytes(pieces(prompt, g, NX - 1), s2_ss.at[g])
            for root in range(PROMPT):
                @pl.when(c != root)
                def _():
                    to_root(g, root).wait_send()

        @pl.when(x > 0)
        def _():
            wait_bytes(st2s.at[g], st2_ss.at[g])
        wait_bytes(pieces(prompt, g, NZ - 1), s3_ss.at[g])
        wait_bytes(st1.at[g, pl.ds(0, NZ - 1)], st1_ss.at[g])

    send_bias()
    finish(0)
    step1(1)
    bias1()
    drain(0)
    step2(1)
    bias2()
    finish(1)

    @pl.when(is_root)
    def _():
        loop(0, GROUPS, finish_root)
    bias3()
    drain(1)
    wait_bytes(b1.at[pl.ds(0, NZ - 1)], b1_ss)
    wait_bytes(b2.at[pl.ds(0, NX - 1)], b2_ss)
    wait_bytes(b3.at[pl.ds(0, 2 * NY - 1)], b3_ss)


def hand_out(dq, dk, dv, db, dq_out, dk_out, dv_out, db_out, sems):
    copies = [pltpu.make_async_copy(a, b, sems.at[i])
              for i, (a, b) in enumerate(((dq, dq_out), (dk, dk_out), (dv, dv_out), (db, db_out)))]
    for copy in copies:
        copy.start()
    for copy in copies:
        copy.wait()


def body(query_in, key_in, value_rows_input, grad_out, query_bias, key_blocks, trace_len):
    any_ = pl.BlockSpec(memory_space=pl.ANY)
    vmem = pl.BlockSpec(memory_space=pltpu.VMEM)
    smem = pl.BlockSpec(memory_space=pltpu.SMEM)
    dma = pltpu.SemaphoreType.DMA
    tile = (2, BLOCK, 128)
    G = GROUPS

    def many(*dims):
        return pltpu.VMEM(dims + tile, BF)
    part = (PROMPT, 2, PIECE, 128)
    dq, dk, dv, db = pl.pallas_call(
        kernel,
        out_shape=(
            pltpu.VMEM((2 * BLOCK, 4096), BF),
            pltpu.VMEM((2 * BLOCK, 512), BF),
            pltpu.VMEM((2 * BLOCK, 512), BF),
            pltpu.VMEM((32, 128), F32),
        ),
        in_specs=[any_, any_, any_, any_, vmem, smem, smem],
        out_specs=(vmem, vmem, vmem, vmem),
        scratch_shapes=[
            pltpu.VMEM((2, G, 2 * BLOCK, 1024), BF), pltpu.VMEM((2, G, 2 * BLOCK, 1024), BF),
            many(2, 4), many(G, PROMPT), many(2, G, NEAR),
            pltpu.VMEM((2, G, NEAR) + tile, F32), pltpu.VMEM((G, PROMPT) + tile, F32),
            pltpu.VMEM((G, 2 * BLOCK, 1024), BF),
            many(2, G, WINDOW), many(2, G, 2, 2), many(G, 2), many(2, G), many(2, G),
            many(G, PROMPT),
            pltpu.VMEM((G, NZ) + part, BF), pltpu.VMEM((G,) + part, BF), pltpu.VMEM((G, NX) + part, BF),
            pltpu.VMEM((G,) + part, BF), pltpu.VMEM((G, 2 * NZ, 2, PIECE, 128), BF),
            pltpu.VMEM((G, 8, 128), F32), pltpu.VMEM((NZ, G, 8, 128), F32),
            pltpu.VMEM((G, 8, 128), F32), pltpu.VMEM((NX, G, 8, 128), F32),
            pltpu.VMEM((G, 8, 128), F32), pltpu.VMEM((2 * NY, G, 8, 128), F32),
            dma((G,)), dma((G,)), dma((2, 2, 4)), dma((2, 2, G)),
            dma((G,)), dma((G,)), dma((G,)), dma((G,)), dma((2, G)), dma((2, G)),
            dma((2, G, 2, 2)), dma((2, G, WINDOW)),
            dma((G,)), dma((G, PROMPT)), dma((G,)), dma((G,)), dma((G,)), dma((G,)), dma((G, 2)), dma((G, 2)),
            dma((2, G, WINDOW)), dma((2, G, 2, 2)), dma((G, 2)), dma((2, G)), dma((2, G)),
            dma((G,)), dma((G,)), dma((G,)), dma((G,)), dma((G, PROMPT)), dma((G,)),
            dma, dma, dma, dma, dma, dma,
        ],
        compiler_params=pltpu.CompilerParams(
            collective_id=0, has_side_effects=True, vmem_limit_bytes=58 * 2**20),
        name="attention",
    )(query_in[0], key_in[0], value_rows_input[0], grad_out[0], query_bias.reshape(32, 128),
      key_blocks.transpose(2, 0, 1), trace_len)
    dq, dk, dv, db = pl.pallas_call(
        hand_out,
        out_shape=(
            jax.ShapeDtypeStruct((2 * BLOCK, 4096), BF),
            jax.ShapeDtypeStruct((2 * BLOCK, 512), BF),
            jax.ShapeDtypeStruct((2 * BLOCK, 512), BF),
            jax.ShapeDtypeStruct((32, 128), F32),
        ),
        in_specs=[vmem] * 4,
        out_specs=(any_,) * 4,
        scratch_shapes=[dma((4,))],
        compiler_params=pltpu.CompilerParams(has_side_effects=True),
        name="hand_out",
    )(*(pltpu.with_memory_space_constraint(a, pltpu.VMEM) for a in (dq, dk, dv, db)))
    return dq[None], dk[None], dv[None], db.reshape(4096)


def solution(mesh):
    return jax.shard_map(
        body,
        mesh=mesh,
        in_specs=(
            P("dp", "ctx", None),
            P("dp", "ctx", None),
            P("dp", "ctx", None),
            P("dp", "ctx", None),
            P(),
            P("dp", None, None),
            P("dp"),
        ),
        out_specs=(P("dp", "ctx", None), P("dp", "ctx", None), P("dp", "ctx", None), P()),
        check_vma=False,
    )
```

```python
import math

import jax
import jax.numpy as jnp
from jax import lax
from jax.experimental import pallas as pl
from jax.experimental.pallas import tpu as pltpu
from jax.sharding import PartitionSpec as P

HEAD_SIZE = 128
BLOCK = 128
PROMPT = 2
WINDOW = 3
NBLK = 128
N_CTX = 64
CHIPS = 32
NZ, NX, NY = 8, 4, 4
GROUPS = 2
PER_GROUP = 8
PIECE = BLOCK // NZ
SLOTS = PROMPT + WINDOW + 1
NEAR = 5
ROWS = 65536
SCALE = HEAD_SIZE ** (-0.5)
SCALE2 = SCALE * math.log2(math.e)
FAR = -1e30
BF, F32 = jnp.bfloat16, jnp.float32
MESH = pl.DeviceIdType.MESH


def dot(a, b, ca, cb):
    return lax.dot_general(a, b, (((ca,), (cb,)), ((), ())), preferred_element_type=F32)


def kernel(q_hbm, k_hbm, v_hbm, go_hbm, bias_ref, kb_ref, tl_ref,
           dq_ref, dk_ref, dv_ref, db_ref,
           qv, gv, stage, prompt, cand, acc, pacc, dqs, ret_s, ret_r, refl_r, sib_s, sib_r,
           ps, st1, st2s, st2, st3s, st3, bsrc, b1, b2s, b2, b3s, b3,
           q_sem, g_sem, kv_sem, own_sem, qx_ss, qx_rs, gx_ss, gx_rs, cx_ss, cx_rs,
           win_ss, win_rs, s1_ss, s1_rs, s2_ss, s2_rs, s3_ss, s3_rs, dq_ss, dq_rs, do_sem,
           ret_ss, ret_rs, refl_rs, sib_ss, sib_rs, st1_ss, st1_rs, st2_ss, st2_rs, st3_ss, st3_rs,
           b1_ss, b1_rs, b2_ss, b2_rs, b3_ss, b3_rs):
    c = lax.axis_index("ctx")
    y = lax.axis_index("dp")
    core = lax.rem(c, 2)
    other = 1 - core
    chip = c // 2
    x = lax.rem(chip, NX)
    z = chip // NX
    sibling = chip * 2 + other
    is_root = c < PROMPT

    def at(zz, xx, rr):
        return (zz * NX + xx) * 2 + rr

    def rcopy(src, dst, ss, rs, dev):
        return pltpu.make_async_remote_copy(src_ref=src, dst_ref=dst, send_sem=ss, recv_sem=rs,
                                            device_id={"ctx": dev}, device_id_type=MESH)

    def wait_bytes(ref, sem):
        pltpu.make_async_copy(ref, ref, sem).wait()

    def loop(lo, hi, f):
        def step(i, carry):
            f(i)
            return carry
        lax.fori_loop(lo, hi, step, 0)

    def span(start, size):
        return pl.ds(pl.multiple_of(start, size), size)

    def kv_copy(half, kv, head, dst, sem):
        src = k_hbm if kv == 0 else v_hbm
        return pltpu.make_async_copy(src.at[half * BLOCK:(half + 1) * BLOCK, span(head * 128, 128)], dst, sem)

    def mine(half):
        return other if half == 0 else core

    def kv_stage(half, kv, head):
        return kv_copy(half, kv, head, stage.at[half, head, kv], kv_sem.at[half, kv, head])

    def kv_own(half, kv, g):
        return kv_copy(half, kv, core * 2 + g, cand.at[half, g, mine(half), kv], own_sem.at[half, kv, g])

    def q_own(src, dst, sem, g):
        return pltpu.make_async_copy(src.at[:, span(core * 2048 + g * 1024, 1024)], dst.at[1, g], sem.at[g])

    def q_cross(src, dst, ss, rs, g):
        return rcopy(src.at[:, span(other * 2048 + g * 1024, 1024)], dst.at[0, g], ss.at[g], rs.at[g], sibling)

    def start_stage(h):
        for half in range(2):
            for kv in range(2):
                kv_stage(half, kv, h).start()
    loop(0, 4, start_stage)

    def start_own(g):
        for half in range(2):
            for kv in range(2):
                kv_own(half, kv, g).start()
        q_own(q_hbm, qv, q_sem, g).start()
        q_own(go_hbm, gv, g_sem, g).start()
    loop(0, GROUPS, start_own)

    barrier = pltpu.get_barrier_semaphore()

    def greet(dev, yy):
        pl.semaphore_signal(barrier, inc=1, device_id={"ctx": dev, "dp": yy}, device_id_type=MESH)

    def greet_near(k):
        away = lax.rem(chip + CHIPS - 2 + k, CHIPS)

        @pl.when(k != 2)
        def _():
            greet(away * 2, y)
            greet(away * 2 + 1, y)
    loop(0, 5, greet_near)

    gi = z * 2 + core

    def greet_group(k):
        j = lax.rem(gi + k, 16)
        greet(at(j // 2, x, lax.rem(j, 2)), y)
    loop(1, 16, greet_group)

    def greet_row(k):
        greet(at(z, lax.rem(x + k, NX), core), y)
    loop(1, NX, greet_row)

    def greet_y(k):
        yy = lax.rem(y + k, NY)
        greet(c, yy)
        greet(sibling, yy)
    loop(1, NY, greet_y)

    def zero(g):
        for half in range(2):
            ret_r[half, g] = jnp.zeros((2, 2, 2, BLOCK, 128), BF)
            acc[half, g] = jnp.zeros((NEAR, 2, BLOCK, 128), F32)
        refl_r[g] = jnp.zeros((2, 2, BLOCK, 128), BF)
        pacc[g] = jnp.zeros((PROMPT, 2, BLOCK, 128), F32)
        bsrc[g] = jnp.zeros((8, 128), F32)
    loop(0, GROUPS, zero)

    def wait_stage(h):
        for half in range(2):
            for kv in range(2):
                kv_stage(half, kv, h).wait()
    loop(0, 4, wait_stage)

    pl.semaphore_wait(barrier, 8 + 15 + 3 + 6)

    def rows16(p):
        return span(p * PIECE, PIECE)

    def scatter_prompt(g):
        @pl.when(is_root)
        def _():
            prompt[g, c, :, 0:PIECE, :] = stage[0, c * 2 + g, :, 0:PIECE, :]

            def scatter(k):
                j = lax.rem(c + k, 16)
                p, r = j // 2, lax.rem(j, 2)
                rcopy(stage.at[0, r * 2 + g, :, rows16(p), :], prompt.at[g, c, :, rows16(p), :],
                      s1_ss.at[g], s1_rs.at[g, c], at(p, 0, r)).start()
            loop(1, 16, scatter)
    scatter_prompt(0)

    def win_low(g, r, far):
        dst = lax.rem(chip + 1 + far, CHIPS) * 2 + r
        slot = 4 if far else 1 + 2 - core
        return rcopy(stage.at[0, r * 2 + g], cand.at[0, g, slot], win_ss.at[0, g, r, far], win_rs.at[0, g, slot - 2], dst)

    def win_up(g, r, far):
        dst = (chip - 1 - far) * 2 + r
        slot = 4 if far else 1 + 1 + core
        return rcopy(stage.at[1, r * 2 + g], cand.at[1, g, slot], win_ss.at[1, g, r, far], win_rs.at[1, g, slot - 2], dst)

    def win_fold(g, r):
        return rcopy(stage.at[0, r * 2 + g], cand.at[1, g, 4], win_ss.at[1, g, r, 1], win_rs.at[1, g, 2],
                     N_CTX - 4 + r)

    def cross(half, g):
        slot = mine(half)
        return rcopy(stage.at[half, other * 2 + g], cand.at[half, g, slot], cx_ss.at[half, g], cx_rs.at[half, g], sibling)

    def each_near(g, act):
        for r in range(2):
            act(win_low(g, r, 0))

            @pl.when(chip >= 1)
            def _():
                act(win_up(g, r, 0))
        for half in range(2):
            act(cross(half, g))
        act(q_cross(q_hbm, qv, qx_ss, qx_rs, g))
        act(q_cross(go_hbm, gv, gx_ss, gx_rs, g))

    def each_far(g, act):
        for r in range(2):
            @pl.when(core == 1)
            def _():
                act(win_low(g, r, 1))

            @pl.when((core == 0) & (chip >= 2))
            def _():
                act(win_up(g, r, 1))

            @pl.when(c == N_CTX - 1)
            def _():
                act(win_fold(g, r))

    def wait_slots(g, half, slots):
        for slot in slots:
            rcopy(cand.at[half, g, slot], cand.at[half, g, slot], win_ss.at[0, g, 0, 0], win_rs.at[half, g, slot - 2],
                  sibling).wait_recv()

    def prompt_piece(g):
        return prompt.at[g, :, :, rows16(z), :]

    def prompt_row(g):
        @pl.when(x == 0)
        def _():
            for r in range(PROMPT):
                @pl.when(c != r)
                def _():
                    wait_bytes(prompt.at[g, r, :, rows16(z), :], s1_rs.at[g, r])

            def send(k):
                rcopy(prompt_piece(g), prompt_piece(g), s2_ss.at[g], s2_rs.at[g], at(z, k, core)).start()
            loop(1, NX, send)

    def prompt_column(g):
        @pl.when(x > 0)
        def _():
            wait_bytes(prompt_piece(g), s2_rs.at[g])

        def send(k):
            rcopy(prompt_piece(g), prompt_piece(g), s3_ss.at[g], s3_rs.at[g], at(lax.rem(z + k, NZ), x, core)).start()
        loop(1, NZ, send)

    def pieces(ref, g, n):
        return ref.at[g, :, :, pl.ds(0, n * PIECE), :]

    each_near(0, lambda copy: copy.start())
    prompt_row(0)
    prompt_column(0)
    each_far(0, lambda copy: copy.start())

    width = PER_GROUP * 128
    kk = lax.broadcasted_iota(jnp.int32, (BLOCK, width), 0)
    qi = lax.rem(lax.broadcasted_iota(jnp.int32, (BLOCK, width), 1), BLOCK)
    lane = lax.rem(lax.broadcasted_iota(jnp.int32, (1, width), 1), BLOCK)
    length = tl_ref[0]

    def unit(g, half, turn, leave=None):
        rho = 1 - turn
        role = other if turn else core
        dev = chip * 2 + rho
        blk = jnp.where(half == 0, dev, NBLK - 1 - dev)
        base = jnp.where(half == 0, turn, rho)
        rows = span(half * BLOCK, BLOCK)
        bias = bias_ref[span(core * 16 + g * 8, 8), :]
        Q = jnp.concatenate(
            [(qv[role, g, rows, j * 128:(j + 1) * 128].astype(F32) + bias[j:j + 1]).astype(BF)
             for j in range(PER_GROUP)], 0)
        G = jnp.concatenate([gv[role, g, rows, j * 128:(j + 1) * 128] for j in range(PER_GROUP)], 0)
        K, V = (jnp.concatenate(
            [prompt[g, s, kv] for s in range(PROMPT)] + [cand[half, g, base + d, kv] for d in range(WINDOW + 1)], 0)
            for kv in range(2))
        off = [jnp.where(kb_ref[s, 0, blk] >= 0, 0.0, FAR).astype(F32) for s in range(SLOTS)]
        S = dot(K, Q, 1, 1)
        parts, m = [], None
        for s in range(SLOTS):
            v = S[s * 128:(s + 1) * 128]
            if s == PROMPT:
                v = jnp.where(kk <= qi, v, FAR)
            parts.append(v)
            mm = jnp.max(v, 0, keepdims=True) + off[s]
            m = mm if m is None else jnp.maximum(m, mm)
        m = m * SCALE2
        exps, tot = [], None
        for s in range(SLOTS):
            p = jnp.exp2(parts[s] * SCALE2 - (m - off[s]))
            exps.append(p)
            t = jnp.sum(p, 0, keepdims=True)
            tot = t if tot is None else tot + t
        inv = jnp.where(blk * BLOCK + lane < length, 1.0 / tot, 0.0)
        probs = jnp.concatenate(exps, 0) * inv
        low = probs.astype(BF)
        dP = dot(V, G, 1, 1)
        r = jnp.sum(probs * dP, 0, keepdims=True)
        dS = (probs * (dP - r)).astype(BF)
        dv = dot(low, G, 1, 0)
        dk = dot(dS, Q, 1, 0) * SCALE
        for kv, val in ((0, dk), (1, dv)):
            for s in range(PROMPT):
                pacc[g, s, kv] = pacc[g, s, kv] + val[s * 128:(s + 1) * 128]
            for d in range(WINDOW + 1):
                acc[half, g, base + d, kv] = acc[half, g, base + d, kv] + val[256 + d * 128:384 + d * 128]
        if leave is not None:
            leave()
        dq = dot(dS, K, 0, 0)
        for j in range(PER_GROUP):
            t = dq[j * 128:(j + 1) * 128] * SCALE
            dqs[role, g, rows, j * 128:(j + 1) * 128] = t.astype(BF)
            bsrc[g, j:j + 1, :] = bsrc[g, j:j + 1, :] + jnp.sum(t, 0, keepdims=True)

    def dq_cross(g, half):
        rows = span(half * BLOCK, BLOCK)
        return rcopy(dqs.at[0, g, rows, :], dq_ref.at[rows, span(core * 2048 + g * 1024, 1024)],
                     dq_ss.at[g, half], dq_rs.at[g, half], sibling)

    def dq_own(g, half):
        rows = span(half * BLOCK, BLOCK)
        return pltpu.make_async_copy(dqs.at[1, g, rows, :], dq_ref.at[rows, span(core * 2048 + g * 1024, 1024)],
                                     do_sem.at[g, half])

    def dq_leave(g, half, turn):
        @pl.when(core == turn)
        def _():
            dq_cross(g, half).start()

        @pl.when(core != turn)
        def _():
            dq_own(g, half).start()

    def ret_low(g, e):
        far = 1 if e == 3 else 0
        return rcopy(ret_s.at[0, g, e - 1], ret_r.at[0, g, core, far], ret_ss.at[0, g, e - 1],
                     ret_rs.at[0, g, core, far], lax.rem(chip * 2 + N_CTX - e, N_CTX))

    def ret_up(g, e):
        far = 1 if e == 3 else 0
        return rcopy(ret_s.at[1, g, e - 1], ret_r.at[1, g, core, far], ret_ss.at[1, g, e - 1],
                     ret_rs.at[1, g, core, far], chip * 2 + 1 + e)

    def ret_fold(g):
        return rcopy(ret_s.at[1, g, 2], refl_r.at[g, core], ret_ss.at[1, g, 2], refl_rs.at[g, core], N_CTX - 1)

    def sib_copy(g, half):
        return rcopy(sib_s.at[half, g], sib_r.at[half, g], sib_ss.at[half, g], sib_rs.at[half, g], sibling)

    def each_low(g, act):
        for e in range(1, WINDOW + 1):
            act(ret_low(g, e))
        act(sib_copy(g, 0))

    def each_up(g, act):
        @pl.when(chip < CHIPS - 1)
        def _():
            for e in range(1, WINDOW):
                act(ret_up(g, e))
        act(sib_copy(g, 1))

    def each_up_far(g, act):
        @pl.when(chip < CHIPS - 2)
        def _():
            act(ret_up(g, WINDOW))

        @pl.when(chip == CHIPS - 2)
        def _():
            act(ret_fold(g))

    def send_up_far(g):
        ret_s[1, g, 2] = acc[1, g, 4].astype(BF)
        each_up_far(g, lambda copy: copy.start())

    def send_low(g):
        for e in range(WINDOW):
            ret_s[0, g, e] = acc[0, g, 2 + e].astype(BF)
        sib_s[0, g] = acc[0, g, core].astype(BF)
        each_low(g, lambda copy: copy.start())

    def send_up(g):
        for e in range(WINDOW - 1):
            ret_s[1, g, e] = acc[1, g, 2 + e].astype(BF)
        sib_s[1, g] = acc[1, g, other].astype(BF)
        each_up(g, lambda copy: copy.start())

    def fold_sums(g):
        for e in range(WINDOW):
            acc[0, g, e] = acc[0, g, e] + acc[1, g, 2 + e]

    def wait_recv(ref, sem):
        rcopy(ref, ref, win_ss.at[0, 0, 0, 0], sem, sibling).wait_recv()

    def wait_ret(g):
        for r in range(2):
            wait_recv(ret_r.at[0, g, r, 0], ret_rs.at[0, g, r, 0])

            @pl.when(core == 1)
            def _():
                wait_recv(ret_r.at[0, g, r, 1], ret_rs.at[0, g, r, 1])

            @pl.when(chip >= 1)
            def _():
                wait_recv(ret_r.at[1, g, r, 0], ret_rs.at[1, g, r, 0])

            @pl.when((core == 0) & (chip >= 2))
            def _():
                wait_recv(ret_r.at[1, g, r, 1], ret_rs.at[1, g, r, 1])

            @pl.when(c == N_CTX - 1)
            def _():
                wait_recv(refl_r.at[g, r], refl_rs.at[g, r])
        for half in range(2):
            wait_recv(sib_r.at[half, g], sib_rs.at[half, g])

    def send_shared(g):
        ps[g] = pacc[g].astype(BF)

        def send(k):
            zj = lax.rem(z + k, NZ)
            dev = at(zj, x, core)
            rcopy(ps.at[g, :, :, rows16(zj), :], st1.at[g, z], st1_ss.at[g], st1_rs.at[g], dev).start()
        loop(1, NZ, send)
        st1[g, z] = ps[g, :, :, rows16(z), :]

    def total_of(ref, g, n):
        total = ref[g, 0].astype(F32)
        for k in range(1, n):
            total = total + ref[g, k].astype(F32)
        return total

    def step1(g):
        wait_bytes(st1.at[g, pl.ds(0, NZ - 1)], st1_rs.at[g])
        st2s[g] = total_of(st1, g, NZ).astype(BF)

        @pl.when(x == 0)
        def _():
            st2[g, 0] = st2s[g]

        @pl.when(x > 0)
        def _():
            rcopy(st2s.at[g], st2.at[g, x], st2_ss.at[g], st2_rs.at[g], at(z, 0, core)).start()
    def to_root(g, root):
        return rcopy(st3s.at[g, root], st3.at[g, core * NZ + z], st3_ss.at[g, root], st3_rs.at[g], root)

    def step2(g):
        @pl.when(x == 0)
        def _():
            wait_bytes(st2.at[g, pl.ds(0, NX - 1)], st2_rs.at[g])
            st3s[g] = total_of(st2, g, NX).astype(BF)
            for root in range(PROMPT):
                @pl.when(c == root)
                def _():
                    st3[g, root * NZ] = st3s[g, root]

                @pl.when(c != root)
                def _():
                    to_root(g, root).start()
    def send_bias():
        def send(k):
            rcopy(bsrc, b1.at[z], b1_ss, b1_rs, at(lax.rem(z + k, NZ), x, core)).start()
        loop(1, NZ, send)
        b1[z] = bsrc[...]

    def sum_bias(ref, n):
        total = ref[0]
        for k in range(1, n):
            total = total + ref[k]
        return total

    def bias1():
        wait_bytes(b1.at[pl.ds(0, NZ - 1)], b1_rs)
        total = sum_bias(b1, NZ)
        b2s[...] = total
        b2[x] = total

        def send(k):
            rcopy(b2s, b2.at[x], b2_ss, b2_rs, at(z, lax.rem(x + k, NX), core)).start()
        loop(1, NX, send)

    def bias2():
        wait_bytes(b2.at[pl.ds(0, NX - 1)], b2_rs)
        total = sum_bias(b2, NX)
        b3s[...] = total
        b3[core * NY + y] = total

        def send(k):
            j = lax.rem(core * NY + y + k, 2 * NY)
            pltpu.make_async_remote_copy(
                src_ref=b3s, dst_ref=b3.at[core * NY + y], send_sem=b3_ss, recv_sem=b3_rs,
                device_id={"ctx": chip * 2 + j // NY, "dp": lax.rem(j, NY)}, device_id_type=MESH).start()
        loop(1, 2 * NY, send)

    def bias3():
        wait_bytes(b3.at[pl.ds(0, 2 * NY - 1)], b3_rs)
        for r in range(2):
            total = b3[r * NY]
            for k in range(1, NY):
                total = total + b3[r * NY + k]
            for g in range(GROUPS):
                db_ref[r * 16 + g * 8:r * 16 + g * 8 + 8, :] = total[g] * (1.0 / math.sqrt(ROWS))

    def finish(g):
        wait_ret(g)
        for t in range(2):
            r = other if t else core
            cols = span((r * 2 + g) * 128, 128)
            for half in range(2):
                for kv, out in ((0, dk_ref), (1, dv_ref)):
                    total = sib_r[half, g, kv].astype(F32) if t else acc[half, g, mine(half), kv]
                    for far in range(2):
                        total = total + ret_r[half, g, r, far, kv].astype(F32)
                    if half == 0:
                        total = total + refl_r[g, r, kv].astype(F32)

                        @pl.when(is_root)
                        def _():
                            pacc[g, t, kv] = total
                    out[half * BLOCK:(half + 1) * BLOCK, cols] = total.astype(BF)

    def finish_root(g):
        wait_bytes(st3.at[g, pl.ds(0, 2 * NZ - 1)], st3_rs.at[g])
        for t in range(2):
            r = other if t else core
            cols = span((r * 2 + g) * 128, 128)
            for kv, out in ((0, dk_ref), (1, dv_ref)):
                for p in range(NZ):
                    rr = slice(p * PIECE, (p + 1) * PIECE)
                    out[rr, cols] = (pacc[g, t, kv, rr, :] + st3[g, r * NZ + p, kv].astype(F32)).astype(BF)

    def main(i):
        g, half = i // 2, lax.rem(i, 2)

        @pl.when(half == 0)
        def _():
            for kv in range(2):
                kv_own(0, kv, g).wait()
                kv_own(1, kv, g).wait()
            q_own(q_hbm, qv, q_sem, g).wait()
            q_own(go_hbm, gv, g_sem, g).wait()
            q_cross(q_hbm, qv, qx_ss, qx_rs, g).wait_recv()
            q_cross(go_hbm, gv, gx_ss, gx_rs, g).wait_recv()
            cross(0, g).wait_recv()
            wait_slots(g, 0, (2, 3))
            wait_bytes(pieces(prompt, g, NZ - 1), s3_rs.at[g])

        @pl.when(i == 0)
        def _():
            scatter_prompt(1)
            each_near(1, lambda copy: copy.start())
            each_far(1, lambda copy: copy.start())

        @pl.when(half == 1)
        def _():
            cross(1, g).wait_recv()

            @pl.when(chip < CHIPS - 1)
            def _():
                wait_slots(g, 1, range(2, NEAR))

            @pl.when(chip == CHIPS - 1)
            def _():
                for slot in range(2, NEAR):
                    cand[1, g, slot] = cand[0, g, slot - 2]
        unit(g, half, 0)

        @pl.when(half == 1)
        def _():
            send_up_far(g)
        dq_leave(g, half, 0)

        @pl.when(i == 0)
        def _():
            prompt_row(1)

        @pl.when(i == 2)
        def _():
            step1(0)

        def leave():
            @pl.when(half == 1)
            def _():
                send_shared(g)

                @pl.when(chip == CHIPS - 1)
                def _():
                    fold_sums(g)
                    send_low(g)
                send_up(g)

            @pl.when((half == 0) & (chip < CHIPS - 1))
            def _():
                send_low(g)

        @pl.when(half == 0)
        def _():
            wait_slots(g, 0, (4,))
        unit(g, half, 1, leave)
        dq_leave(g, half, 1)

        @pl.when(i == 0)
        def _():
            prompt_column(1)

        @pl.when(i == 2)
        def _():
            step2(0)
    loop(0, 2 * GROUPS, main)

    def drain(g):
        for half in range(2):
            dq_cross(g, half).wait()
            dq_own(g, half).wait()
        each_near(g, lambda copy: copy.wait_send())
        each_far(g, lambda copy: copy.wait_send())
        each_low(g, lambda copy: copy.wait_send())
        each_up(g, lambda copy: copy.wait_send())
        each_up_far(g, lambda copy: copy.wait_send())

        @pl.when(is_root)
        def _():
            wait_bytes(st3.at[g, pl.ds(0, 2 * NZ - 1)], s1_ss.at[g])

        @pl.when(x == 0)
        def _():
            wait_bytes(pieces(prompt, g, NX - 1), s2_ss.at[g])
            for root in range(PROMPT):
                @pl.when(c != root)
                def _():
                    to_root(g, root).wait_send()

        @pl.when(x > 0)
        def _():
            wait_bytes(st2s.at[g], st2_ss.at[g])
        wait_bytes(pieces(prompt, g, NZ - 1), s3_ss.at[g])
        wait_bytes(st1.at[g, pl.ds(0, NZ - 1)], st1_ss.at[g])

    send_bias()
    finish(0)
    step1(1)
    bias1()
    drain(0)
    step2(1)
    bias2()
    finish(1)

    @pl.when(is_root)
    def _():
        loop(0, GROUPS, finish_root)
    bias3()
    drain(1)
    wait_bytes(b1.at[pl.ds(0, NZ - 1)], b1_ss)
    wait_bytes(b2.at[pl.ds(0, NX - 1)], b2_ss)
    wait_bytes(b3.at[pl.ds(0, 2 * NY - 1)], b3_ss)


def hand_out(dq, dk, dv, db, dq_out, dk_out, dv_out, db_out, sems):
    copies = [pltpu.make_async_copy(a, b, sems.at[i])
              for i, (a, b) in enumerate(((dq, dq_out), (dk, dk_out), (dv, dv_out), (db, db_out)))]
    for copy in copies:
        copy.start()
    for copy in copies:
        copy.wait()


def body(query_in, key_in, value_rows_input, grad_out, query_bias, key_blocks, trace_len):
    any_ = pl.BlockSpec(memory_space=pl.ANY)
    vmem = pl.BlockSpec(memory_space=pltpu.VMEM)
    smem = pl.BlockSpec(memory_space=pltpu.SMEM)
    dma = pltpu.SemaphoreType.DMA
    tile = (2, BLOCK, 128)
    G = GROUPS

    def many(*dims):
        return pltpu.VMEM(dims + tile, BF)
    part = (PROMPT, 2, PIECE, 128)
    dq, dk, dv, db = pl.pallas_call(
        kernel,
        out_shape=(
            pltpu.VMEM((2 * BLOCK, 4096), BF),
            pltpu.VMEM((2 * BLOCK, 512), BF),
            pltpu.VMEM((2 * BLOCK, 512), BF),
            pltpu.VMEM((32, 128), F32),
        ),
        in_specs=[any_, any_, any_, any_, vmem, smem, smem],
        out_specs=(vmem, vmem, vmem, vmem),
        scratch_shapes=[
            pltpu.VMEM((2, G, 2 * BLOCK, 1024), BF), pltpu.VMEM((2, G, 2 * BLOCK, 1024), BF),
            many(2, 4), many(G, PROMPT), many(2, G, NEAR),
            pltpu.VMEM((2, G, NEAR) + tile, F32), pltpu.VMEM((G, PROMPT) + tile, F32),
            pltpu.VMEM((2, G, 2 * BLOCK, 1024), BF),
            many(2, G, WINDOW), many(2, G, 2, 2), many(G, 2), many(2, G), many(2, G),
            many(G, PROMPT),
            pltpu.VMEM((G, NZ) + part, BF), pltpu.VMEM((G,) + part, BF), pltpu.VMEM((G, NX) + part, BF),
            pltpu.VMEM((G,) + part, BF), pltpu.VMEM((G, 2 * NZ, 2, PIECE, 128), BF),
            pltpu.VMEM((G, 8, 128), F32), pltpu.VMEM((NZ, G, 8, 128), F32),
            pltpu.VMEM((G, 8, 128), F32), pltpu.VMEM((NX, G, 8, 128), F32),
            pltpu.VMEM((G, 8, 128), F32), pltpu.VMEM((2 * NY, G, 8, 128), F32),
            dma((G,)), dma((G,)), dma((2, 2, 4)), dma((2, 2, G)),
            dma((G,)), dma((G,)), dma((G,)), dma((G,)), dma((2, G)), dma((2, G)),
            dma((2, G, 2, 2)), dma((2, G, WINDOW)),
            dma((G,)), dma((G, PROMPT)), dma((G,)), dma((G,)), dma((G,)), dma((G,)), dma((G, 2)), dma((G, 2)), dma((G, 2)),
            dma((2, G, WINDOW)), dma((2, G, 2, 2)), dma((G, 2)), dma((2, G)), dma((2, G)),
            dma((G,)), dma((G,)), dma((G,)), dma((G,)), dma((G, PROMPT)), dma((G,)),
            dma, dma, dma, dma, dma, dma,
        ],
        compiler_params=pltpu.CompilerParams(
            collective_id=0, has_side_effects=True, vmem_limit_bytes=58 * 2**20),
        name="attention",
    )(query_in[0], key_in[0], value_rows_input[0], grad_out[0], query_bias.reshape(32, 128),
      key_blocks.transpose(2, 0, 1), trace_len)
    dq, dk, dv, db = pl.pallas_call(
        hand_out,
        out_shape=(
            jax.ShapeDtypeStruct((2 * BLOCK, 4096), BF),
            jax.ShapeDtypeStruct((2 * BLOCK, 512), BF),
            jax.ShapeDtypeStruct((2 * BLOCK, 512), BF),
            jax.ShapeDtypeStruct((32, 128), F32),
        ),
        in_specs=[vmem] * 4,
        out_specs=(any_,) * 4,
        scratch_shapes=[dma((4,))],
        compiler_params=pltpu.CompilerParams(has_side_effects=True),
        name="hand_out",
    )(*(pltpu.with_memory_space_constraint(a, pltpu.VMEM) for a in (dq, dk, dv, db)))
    return dq[None], dk[None], dv[None], db.reshape(4096)


def solution(mesh):
    return jax.shard_map(
        body,
        mesh=mesh,
        in_specs=(
            P("dp", "ctx", None),
            P("dp", "ctx", None),
            P("dp", "ctx", None),
            P("dp", "ctx", None),
            P(),
            P("dp", None, None),
            P("dp"),
        ),
        out_specs=(P("dp", "ctx", None), P("dp", "ctx", None), P("dp", "ctx", None), P()),
        check_vma=False,
    )
```

```python
import math

import jax
import jax.numpy as jnp
from jax import lax
from jax.experimental import pallas as pl
from jax.experimental.pallas import tpu as pltpu
from jax.sharding import PartitionSpec as P

HEAD_SIZE = 128
BLOCK = 128
PROMPT = 2
WINDOW = 3
NBLK = 128
N_CTX = 64
CHIPS = 32
NZ, NX, NY = 8, 4, 4
GROUPS = 2
PER_GROUP = 8
PIECE = BLOCK // NZ
SLOTS = PROMPT + WINDOW + 1
NEAR = 5
ROWS = 65536
SCALE = HEAD_SIZE ** (-0.5)
SCALE2 = SCALE * math.log2(math.e)
FAR = -1e30
BF, F32 = jnp.bfloat16, jnp.float32
MESH = pl.DeviceIdType.MESH


def dot(a, b, ca, cb):
    return lax.dot_general(a, b, (((ca,), (cb,)), ((), ())), preferred_element_type=F32)


def kernel(q_hbm, k_hbm, v_hbm, go_hbm, bias_ref, kb_ref, tl_ref,
           dq_ref, dk_ref, dv_ref, db_ref,
           qv, gv, stage, prompt, cand, acc, pacc, dqs, ret_s, ret_r, refl_r, sib_s, sib_r,
           ps, st1, st2s, st2, st3s, st3, bsrc, b1, b2s, b2, b3s, b3,
           q_sem, g_sem, kv_sem, own_sem, qx_ss, qx_rs, gx_ss, gx_rs, cx_ss, cx_rs,
           win_ss, win_rs, s1_ss, s1_rs, s2_ss, s2_rs, s3_ss, s3_rs, dq_ss, dq_rs,
           ret_ss, ret_rs, refl_rs, sib_ss, sib_rs, st1_ss, st1_rs, st2_ss, st2_rs, st3_ss, st3_rs,
           b1_ss, b1_rs, b2_ss, b2_rs, b3_ss, b3_rs):
    c = lax.axis_index("ctx")
    y = lax.axis_index("dp")
    core = lax.rem(c, 2)
    other = 1 - core
    chip = c // 2
    x = lax.rem(chip, NX)
    z = chip // NX
    sibling = chip * 2 + other
    is_root = c < PROMPT

    def at(zz, xx, rr):
        return (zz * NX + xx) * 2 + rr

    def rcopy(src, dst, ss, rs, dev):
        return pltpu.make_async_remote_copy(src_ref=src, dst_ref=dst, send_sem=ss, recv_sem=rs,
                                            device_id={"ctx": dev}, device_id_type=MESH)

    def wait_bytes(ref, sem):
        pltpu.make_async_copy(ref, ref, sem).wait()

    def loop(lo, hi, f):
        def step(i, carry):
            f(i)
            return carry
        lax.fori_loop(lo, hi, step, 0)

    def each(lo, hi, f):
        for i in range(lo, hi):
            f(i)

    def span(start, size):
        return pl.ds(pl.multiple_of(start, size), size)

    def kv_copy(half, kv, head, dst, sem):
        src = k_hbm if kv == 0 else v_hbm
        return pltpu.make_async_copy(src.at[half * BLOCK:(half + 1) * BLOCK, span(head * 128, 128)], dst, sem)

    def mine(half):
        return other if half == 0 else core

    def kv_stage(half, kv, head):
        return kv_copy(half, kv, head, stage.at[half, head, kv], kv_sem.at[half, kv, head])

    def kv_own(half, kv, g):
        return kv_copy(half, kv, core * 2 + g, cand.at[half, g, mine(half), kv], own_sem.at[half, kv, g])

    def q_own(src, dst, sem, g):
        return pltpu.make_async_copy(src.at[:, span(core * 2048 + g * 1024, 1024)], dst.at[1, g], sem.at[g])

    def q_cross(src, dst, ss, rs, g):
        return rcopy(src.at[:, span(other * 2048 + g * 1024, 1024)], dst.at[0, g], ss.at[g], rs.at[g], sibling)

    def start_stage(h):
        for half in range(2):
            for kv in range(2):
                kv_stage(half, kv, h).start()
    loop(0, 4, start_stage)

    def start_own(g):
        for half in range(2):
            for kv in range(2):
                kv_own(half, kv, g).start()
        q_own(q_hbm, qv, q_sem, g).start()
        q_own(go_hbm, gv, g_sem, g).start()
    loop(0, GROUPS, start_own)

    barrier = pltpu.get_barrier_semaphore()

    def greet(dev, yy):
        pl.semaphore_signal(barrier, inc=1, device_id={"ctx": dev, "dp": yy}, device_id_type=MESH)

    def greet_near(k):
        away = lax.rem(chip + CHIPS - 2 + k, CHIPS)

        @pl.when(k != 2)
        def _():
            greet(away * 2, y)
            greet(away * 2 + 1, y)
    loop(0, 5, greet_near)

    gi = z * 2 + core

    def greet_group(k):
        j = lax.rem(gi + k, 16)
        greet(at(j // 2, x, lax.rem(j, 2)), y)
    loop(1, 16, greet_group)

    def greet_row(k):
        greet(at(z, lax.rem(x + k, NX), core), y)
    loop(1, NX, greet_row)

    def greet_y(k):
        yy = lax.rem(y + k, NY)
        greet(c, yy)
        greet(sibling, yy)
    loop(1, NY, greet_y)

    def zero(g):
        for half in range(2):
            ret_r[half, g] = jnp.zeros((2, 2, 2, BLOCK, 128), BF)
            acc[half, g] = jnp.zeros((NEAR, 2, BLOCK, 128), F32)
        refl_r[g] = jnp.zeros((2, 2, BLOCK, 128), BF)
        pacc[g] = jnp.zeros((PROMPT, 2, BLOCK, 128), F32)
        bsrc[g] = jnp.zeros((8, 128), F32)
    loop(0, GROUPS, zero)

    def wait_stage(h):
        for half in range(2):
            for kv in range(2):
                kv_stage(half, kv, h).wait()
    loop(0, 4, wait_stage)

    pl.semaphore_wait(barrier, 8 + 15 + 3 + 6)

    def rows16(p):
        return span(p * PIECE, PIECE)

    def scatter_prompt(g):
        @pl.when(is_root)
        def _():
            prompt[g, c, :, 0:PIECE, :] = stage[0, c * 2 + g, :, 0:PIECE, :]

            def scatter(k):
                j = lax.rem(c + k, 16)
                p, r = j // 2, lax.rem(j, 2)
                rcopy(stage.at[0, r * 2 + g, :, rows16(p), :], prompt.at[g, c, :, rows16(p), :],
                      s1_ss.at[g], s1_rs.at[g, c], at(p, 0, r)).start()
            loop(1, 16, scatter)
    scatter_prompt(0)

    def win_low(g, r, far):
        dst = lax.rem(chip + 1 + far, CHIPS) * 2 + r
        slot = 4 if far else 1 + 2 - core
        return rcopy(stage.at[0, r * 2 + g], cand.at[0, g, slot], win_ss.at[0, g, r, far], win_rs.at[0, g, slot - 2], dst)

    def win_up(g, r, far):
        dst = (chip - 1 - far) * 2 + r
        slot = 4 if far else 1 + 1 + core
        return rcopy(stage.at[1, r * 2 + g], cand.at[1, g, slot], win_ss.at[1, g, r, far], win_rs.at[1, g, slot - 2], dst)

    def win_fold(g, r):
        return rcopy(stage.at[0, r * 2 + g], cand.at[1, g, 4], win_ss.at[1, g, r, 1], win_rs.at[1, g, 2],
                     N_CTX - 4 + r)

    def cross(half, g):
        slot = mine(half)
        return rcopy(stage.at[half, other * 2 + g], cand.at[half, g, slot], cx_ss.at[half, g], cx_rs.at[half, g], sibling)

    def each_window(g, act):
        for r in range(2):
            act(win_low(g, r, 0))

            @pl.when(chip >= 1)
            def _():
                act(win_up(g, r, 0))

            @pl.when(core == 1)
            def _():
                act(win_low(g, r, 1))

            @pl.when((core == 0) & (chip >= 2))
            def _():
                act(win_up(g, r, 1))

            @pl.when(c == N_CTX - 1)
            def _():
                act(win_fold(g, r))
        for half in range(2):
            act(cross(half, g))
        act(q_cross(q_hbm, qv, qx_ss, qx_rs, g))
        act(q_cross(go_hbm, gv, gx_ss, gx_rs, g))

    def wait_near(g, half):
        cross(half, g).wait_recv()
        for slot in range(2, NEAR):
            rcopy(cand.at[half, g, slot], cand.at[half, g, slot], win_ss.at[0, g, 0, 0], win_rs.at[half, g, slot - 2],
                  sibling).wait_recv()

    def prompt_piece(g):
        return prompt.at[g, :, :, rows16(z), :]

    def prompt_row(g):
        @pl.when(x == 0)
        def _():
            for r in range(PROMPT):
                @pl.when(c != r)
                def _():
                    wait_bytes(prompt.at[g, r, :, rows16(z), :], s1_rs.at[g, r])

            def send(k):
                rcopy(prompt_piece(g), prompt_piece(g), s2_ss.at[g], s2_rs.at[g], at(z, k, core)).start()
            each(1, NX, send)

    def prompt_column(g):
        @pl.when(x > 0)
        def _():
            wait_bytes(prompt_piece(g), s2_rs.at[g])

        def send(k):
            rcopy(prompt_piece(g), prompt_piece(g), s3_ss.at[g], s3_rs.at[g], at(lax.rem(z + k, NZ), x, core)).start()
        each(1, NZ, send)

    def pieces(ref, g, n):
        return ref.at[g, :, :, pl.ds(0, n * PIECE), :]

    each_window(0, lambda copy: copy.start())
    prompt_row(0)
    prompt_column(0)

    width = PER_GROUP * 128
    kk = lax.broadcasted_iota(jnp.int32, (BLOCK, width), 0)
    qi = lax.rem(lax.broadcasted_iota(jnp.int32, (BLOCK, width), 1), BLOCK)
    lane = lax.rem(lax.broadcasted_iota(jnp.int32, (1, width), 1), BLOCK)
    length = tl_ref[0]

    def unit(g, half, role, leave=None):
        rho = core if role else other
        dev = chip * 2 + rho
        blk = jnp.where(half == 0, dev, NBLK - 1 - dev)
        base = jnp.where(half == 0, 1 - rho, rho)
        rows = span(half * BLOCK, BLOCK)
        bias = bias_ref[span(core * 16 + g * 8, 8), :]
        Q = jnp.concatenate(
            [(qv[role, g, rows, j * 128:(j + 1) * 128].astype(F32) + bias[j:j + 1]).astype(BF)
             for j in range(PER_GROUP)], 0)
        G = jnp.concatenate([gv[role, g, rows, j * 128:(j + 1) * 128] for j in range(PER_GROUP)], 0)
        K, V = (jnp.concatenate(
            [prompt[g, s, kv] for s in range(PROMPT)] + [cand[half, g, base + d, kv] for d in range(WINDOW + 1)], 0)
            for kv in range(2))
        off = [jnp.where(kb_ref[s, 0, blk] >= 0, 0.0, FAR).astype(F32) for s in range(SLOTS)]
        S = dot(K, Q, 1, 1)
        parts, m = [], None
        for s in range(SLOTS):
            v = S[s * 128:(s + 1) * 128]
            if s == PROMPT:
                v = jnp.where(kk <= qi, v, FAR)
            parts.append(v)
            mm = jnp.max(v, 0, keepdims=True) + off[s]
            m = mm if m is None else jnp.maximum(m, mm)
        m = m * SCALE2
        exps, tot = [], None
        for s in range(SLOTS):
            p = jnp.exp2(parts[s] * SCALE2 - (m - off[s]))
            exps.append(p)
            t = jnp.sum(p, 0, keepdims=True)
            tot = t if tot is None else tot + t
        inv = jnp.where(blk * BLOCK + lane < length, 1.0 / tot, 0.0)
        probs = jnp.concatenate(exps, 0) * inv
        low = probs.astype(BF)
        dP = dot(V, G, 1, 1)
        r = jnp.sum(probs * dP, 0, keepdims=True)
        dS = (probs * (dP - r)).astype(BF)
        dv = dot(low, G, 1, 0)
        dk = dot(dS, Q, 1, 0) * SCALE
        for kv, val in ((0, dk), (1, dv)):
            for s in range(PROMPT):
                pacc[g, s, kv] = pacc[g, s, kv] + val[s * 128:(s + 1) * 128]
            for d in range(WINDOW + 1):
                acc[half, g, base + d, kv] = acc[half, g, base + d, kv] + val[256 + d * 128:384 + d * 128]
        if leave is not None:
            leave()
        dq = dot(dS, K, 0, 0)
        for j in range(PER_GROUP):
            t = dq[j * 128:(j + 1) * 128] * SCALE
            if role:
                dq_ref[rows, span(core * 2048 + g * 1024 + j * 128, 128)] = t.astype(BF)
            else:
                dqs[g, rows, j * 128:(j + 1) * 128] = t.astype(BF)
            bsrc[g, j:j + 1, :] = bsrc[g, j:j + 1, :] + jnp.sum(t, 0, keepdims=True)

    def dq_cross(g, half):
        rows = span(half * BLOCK, BLOCK)
        return rcopy(dqs.at[g, rows, :], dq_ref.at[rows, span(core * 2048 + g * 1024, 1024)],
                     dq_ss.at[g, half], dq_rs.at[g, half], sibling)

    def ret_low(g, e):
        far = 1 if e == 3 else 0
        return rcopy(ret_s.at[0, g, e - 1], ret_r.at[0, g, core, far], ret_ss.at[0, g, e - 1],
                     ret_rs.at[0, g, core, far], lax.rem(chip * 2 + N_CTX - e, N_CTX))

    def ret_up(g, e):
        far = 1 if e == 3 else 0
        return rcopy(ret_s.at[1, g, e - 1], ret_r.at[1, g, core, far], ret_ss.at[1, g, e - 1],
                     ret_rs.at[1, g, core, far], chip * 2 + 1 + e)

    def ret_fold(g):
        return rcopy(ret_s.at[1, g, 2], refl_r.at[g, core], ret_ss.at[1, g, 2], refl_rs.at[g, core], N_CTX - 1)

    def sib_copy(g, half):
        return rcopy(sib_s.at[half, g], sib_r.at[half, g], sib_ss.at[half, g], sib_rs.at[half, g], sibling)

    def each_low(g, act):
        for e in range(1, WINDOW + 1):
            act(ret_low(g, e))
        act(sib_copy(g, 0))

    def each_up(g, act):
        for e in range(1, WINDOW + 1):
            @pl.when(chip * 2 + 1 + e < N_CTX)
            def _():
                act(ret_up(g, e))

        @pl.when(chip == CHIPS - 2)
        def _():
            act(ret_fold(g))
        act(sib_copy(g, 1))

    def send_low(g):
        for e in range(WINDOW):
            ret_s[0, g, e] = acc[0, g, 2 + e].astype(BF)
        sib_s[0, g] = acc[0, g, core].astype(BF)
        each_low(g, lambda copy: copy.start())

    def send_up(g):
        for e in range(WINDOW):
            ret_s[1, g, e] = acc[1, g, 2 + e].astype(BF)
        sib_s[1, g] = acc[1, g, other].astype(BF)
        each_up(g, lambda copy: copy.start())

    def fold_sums(g):
        for e in range(WINDOW):
            acc[0, g, e] = acc[0, g, e] + acc[1, g, 2 + e]

    def wait_recv(ref, sem):
        rcopy(ref, ref, win_ss.at[0, 0, 0, 0], sem, sibling).wait_recv()

    def wait_ret(g):
        for r in range(2):
            wait_recv(ret_r.at[0, g, r, 0], ret_rs.at[0, g, r, 0])

            @pl.when(core == 1)
            def _():
                wait_recv(ret_r.at[0, g, r, 1], ret_rs.at[0, g, r, 1])

            @pl.when(chip >= 1)
            def _():
                wait_recv(ret_r.at[1, g, r, 0], ret_rs.at[1, g, r, 0])

            @pl.when((core == 0) & (chip >= 2))
            def _():
                wait_recv(ret_r.at[1, g, r, 1], ret_rs.at[1, g, r, 1])

            @pl.when(c == N_CTX - 1)
            def _():
                wait_recv(refl_r.at[g, r], refl_rs.at[g, r])
        for half in range(2):
            wait_recv(sib_r.at[half, g], sib_rs.at[half, g])

    def send_shared(g):
        ps[g] = pacc[g].astype(BF)

        def send(k):
            zj = lax.rem(z + k, NZ)
            dev = at(zj, x, core)
            rcopy(ps.at[g, :, :, rows16(zj), :], st1.at[g, z], st1_ss.at[g], st1_rs.at[g], dev).start()
        each(1, NZ, send)
        st1[g, z] = ps[g, :, :, rows16(z), :]

    def total_of(ref, g, n):
        total = ref[g, 0].astype(F32)
        for k in range(1, n):
            total = total + ref[g, k].astype(F32)
        return total

    def step1(g):
        wait_bytes(st1.at[g, pl.ds(0, NZ - 1)], st1_rs.at[g])
        st2s[g] = total_of(st1, g, NZ).astype(BF)

        @pl.when(x == 0)
        def _():
            st2[g, 0] = st2s[g]

        @pl.when(x > 0)
        def _():
            rcopy(st2s.at[g], st2.at[g, x], st2_ss.at[g], st2_rs.at[g], at(z, 0, core)).start()
    def to_root(g, root):
        return rcopy(st3s.at[g, root], st3.at[g, core * NZ + z], st3_ss.at[g, root], st3_rs.at[g], root)

    def step2(g):
        @pl.when(x == 0)
        def _():
            wait_bytes(st2.at[g, pl.ds(0, NX - 1)], st2_rs.at[g])
            st3s[g] = total_of(st2, g, NX).astype(BF)
            for root in range(PROMPT):
                @pl.when(c == root)
                def _():
                    st3[g, root * NZ] = st3s[g, root]

                @pl.when(c != root)
                def _():
                    to_root(g, root).start()
    def send_bias():
        def send(k):
            rcopy(bsrc, b1.at[z], b1_ss, b1_rs, at(lax.rem(z + k, NZ), x, core)).start()
        each(1, NZ, send)
        b1[z] = bsrc[...]

    def sum_bias(ref, n):
        total = ref[0]
        for k in range(1, n):
            total = total + ref[k]
        return total

    def bias1():
        wait_bytes(b1.at[pl.ds(0, NZ - 1)], b1_rs)
        total = sum_bias(b1, NZ)
        b2s[...] = total
        b2[x] = total

        def send(k):
            rcopy(b2s, b2.at[x], b2_ss, b2_rs, at(z, lax.rem(x + k, NX), core)).start()
        each(1, NX, send)

    def bias2():
        wait_bytes(b2.at[pl.ds(0, NX - 1)], b2_rs)
        total = sum_bias(b2, NX)
        b3s[...] = total
        b3[core * NY + y] = total

        def send(k):
            j = lax.rem(core * NY + y + k, 2 * NY)
            pltpu.make_async_remote_copy(
                src_ref=b3s, dst_ref=b3.at[core * NY + y], send_sem=b3_ss, recv_sem=b3_rs,
                device_id={"ctx": chip * 2 + j // NY, "dp": lax.rem(j, NY)}, device_id_type=MESH).start()
        each(1, 2 * NY, send)

    def bias3():
        wait_bytes(b3.at[pl.ds(0, 2 * NY - 1)], b3_rs)
        for r in range(2):
            total = b3[r * NY]
            for k in range(1, NY):
                total = total + b3[r * NY + k]
            for g in range(GROUPS):
                db_ref[r * 16 + g * 8:r * 16 + g * 8 + 8, :] = total[g] * (1.0 / math.sqrt(ROWS))

    def finish(g):
        wait_ret(g)
        for t in range(2):
            r = other if t else core
            cols = span((r * 2 + g) * 128, 128)
            for half in range(2):
                for kv, out in ((0, dk_ref), (1, dv_ref)):
                    total = sib_r[half, g, kv].astype(F32) if t else acc[half, g, mine(half), kv]
                    for far in range(2):
                        total = total + ret_r[half, g, r, far, kv].astype(F32)
                    if half == 0:
                        total = total + refl_r[g, r, kv].astype(F32)

                        @pl.when(is_root)
                        def _():
                            pacc[g, t, kv] = total
                    out[half * BLOCK:(half + 1) * BLOCK, cols] = total.astype(BF)

    def finish_root(g):
        wait_bytes(st3.at[g, pl.ds(0, 2 * NZ - 1)], st3_rs.at[g])
        for t in range(2):
            r = other if t else core
            cols = span((r * 2 + g) * 128, 128)
            for kv, out in ((0, dk_ref), (1, dv_ref)):
                for p in range(NZ):
                    rr = slice(p * PIECE, (p + 1) * PIECE)
                    out[rr, cols] = (pacc[g, t, kv, rr, :] + st3[g, r * NZ + p, kv].astype(F32)).astype(BF)

    def main(i):
        g, half = i // 2, lax.rem(i, 2)

        @pl.when(half == 0)
        def _():
            for kv in range(2):
                kv_own(0, kv, g).wait()
                kv_own(1, kv, g).wait()
            q_own(q_hbm, qv, q_sem, g).wait()
            q_own(go_hbm, gv, g_sem, g).wait()
            q_cross(q_hbm, qv, qx_ss, qx_rs, g).wait_recv()
            q_cross(go_hbm, gv, gx_ss, gx_rs, g).wait_recv()
            wait_near(g, 0)
            wait_bytes(pieces(prompt, g, NZ - 1), s3_rs.at[g])

        @pl.when(i == 0)
        def _():
            scatter_prompt(1)
            each_window(1, lambda copy: copy.start())

        @pl.when(half == 1)
        def _():
            cross(1, g).wait_recv()

            @pl.when(chip < CHIPS - 1)
            def _():
                for slot in range(2, NEAR):
                    wait_recv(cand.at[1, g, slot], win_rs.at[1, g, slot - 2])

            @pl.when(chip == CHIPS - 1)
            def _():
                for slot in range(2, NEAR):
                    cand[1, g, slot] = cand[0, g, slot - 2]
        unit(g, half, 0)
        dq_cross(g, half).start()

        @pl.when(i == 0)
        def _():
            prompt_row(1)

        @pl.when(i == 2)
        def _():
            step1(0)

        def leave():
            @pl.when(half == 1)
            def _():
                send_shared(g)

                @pl.when(chip == CHIPS - 1)
                def _():
                    fold_sums(g)
                    send_low(g)
                send_up(g)

            @pl.when((half == 0) & (chip < CHIPS - 1))
            def _():
                send_low(g)
        unit(g, half, 1, leave)

        @pl.when(i == 0)
        def _():
            prompt_column(1)

        @pl.when(i == 2)
        def _():
            step2(0)
    loop(0, 2 * GROUPS, main)

    def drain(g):
        for half in range(2):
            dq_cross(g, half).wait()
        each_window(g, lambda copy: copy.wait_send())
        each_low(g, lambda copy: copy.wait_send())
        each_up(g, lambda copy: copy.wait_send())

        @pl.when(is_root)
        def _():
            wait_bytes(st3.at[g, pl.ds(0, 2 * NZ - 1)], s1_ss.at[g])

        @pl.when(x == 0)
        def _():
            wait_bytes(pieces(prompt, g, NX - 1), s2_ss.at[g])
            for root in range(PROMPT):
                @pl.when(c != root)
                def _():
                    to_root(g, root).wait_send()

        @pl.when(x > 0)
        def _():
            wait_bytes(st2s.at[g], st2_ss.at[g])
        wait_bytes(pieces(prompt, g, NZ - 1), s3_ss.at[g])
        wait_bytes(st1.at[g, pl.ds(0, NZ - 1)], st1_ss.at[g])

    send_bias()
    finish(0)

    @pl.when(is_root)
    def _():
        finish_root(0)
    step1(1)
    bias1()
    drain(0)
    step2(1)
    bias2()
    finish(1)
    drain(1)
    wait_bytes(b1.at[pl.ds(0, NZ - 1)], b1_ss)
    wait_bytes(b2.at[pl.ds(0, NX - 1)], b2_ss)

    @pl.when(is_root)
    def _():
        finish_root(1)
    bias3()
    wait_bytes(b3.at[pl.ds(0, 2 * NY - 1)], b3_ss)


def hand_out(dq, dk, dv, db, dq_out, dk_out, dv_out, db_out, sems):
    copies = [pltpu.make_async_copy(a, b, sems.at[i])
              for i, (a, b) in enumerate(((dq, dq_out), (dk, dk_out), (dv, dv_out), (db, db_out)))]
    for copy in copies:
        copy.start()
    for copy in copies:
        copy.wait()


def body(query_in, key_in, value_rows_input, grad_out, query_bias, key_blocks, trace_len):
    any_ = pl.BlockSpec(memory_space=pl.ANY)
    vmem = pl.BlockSpec(memory_space=pltpu.VMEM)
    smem = pl.BlockSpec(memory_space=pltpu.SMEM)
    dma = pltpu.SemaphoreType.DMA
    tile = (2, BLOCK, 128)
    G = GROUPS

    def many(*dims):
        return pltpu.VMEM(dims + tile, BF)
    part = (PROMPT, 2, PIECE, 128)
    dq, dk, dv, db = pl.pallas_call(
        kernel,
        out_shape=(
            pltpu.VMEM((2 * BLOCK, 4096), BF),
            pltpu.VMEM((2 * BLOCK, 512), BF),
            pltpu.VMEM((2 * BLOCK, 512), BF),
            pltpu.VMEM((32, 128), F32),
        ),
        in_specs=[any_, any_, any_, any_, vmem, smem, smem],
        out_specs=(vmem, vmem, vmem, vmem),
        scratch_shapes=[
            pltpu.VMEM((2, G, 2 * BLOCK, 1024), BF), pltpu.VMEM((2, G, 2 * BLOCK, 1024), BF),
            many(2, 4), many(G, PROMPT), many(2, G, NEAR),
            pltpu.VMEM((2, G, NEAR) + tile, F32), pltpu.VMEM((G, PROMPT) + tile, F32),
            pltpu.VMEM((G, 2 * BLOCK, 1024), BF),
            many(2, G, WINDOW), many(2, G, 2, 2), many(G, 2), many(2, G), many(2, G),
            many(G, PROMPT),
            pltpu.VMEM((G, NZ) + part, BF), pltpu.VMEM((G,) + part, BF), pltpu.VMEM((G, NX) + part, BF),
            pltpu.VMEM((G,) + part, BF), pltpu.VMEM((G, 2 * NZ, 2, PIECE, 128), BF),
            pltpu.VMEM((G, 8, 128), F32), pltpu.VMEM((NZ, G, 8, 128), F32),
            pltpu.VMEM((G, 8, 128), F32), pltpu.VMEM((NX, G, 8, 128), F32),
            pltpu.VMEM((G, 8, 128), F32), pltpu.VMEM((2 * NY, G, 8, 128), F32),
            dma((G,)), dma((G,)), dma((2, 2, 4)), dma((2, 2, G)),
            dma((G,)), dma((G,)), dma((G,)), dma((G,)), dma((2, G)), dma((2, G)),
            dma((2, G, 2, 2)), dma((2, G, WINDOW)),
            dma((G,)), dma((G, PROMPT)), dma((G,)), dma((G,)), dma((G,)), dma((G,)), dma((G, 2)), dma((G, 2)),
            dma((2, G, WINDOW)), dma((2, G, 2, 2)), dma((G, 2)), dma((2, G)), dma((2, G)),
            dma((G,)), dma((G,)), dma((G,)), dma((G,)), dma((G, PROMPT)), dma((G,)),
            dma, dma, dma, dma, dma, dma,
        ],
        compiler_params=pltpu.CompilerParams(
            collective_id=0, has_side_effects=True, vmem_limit_bytes=58 * 2**20),
        name="attention",
    )(query_in[0], key_in[0], value_rows_input[0], grad_out[0], query_bias.reshape(32, 128),
      key_blocks.transpose(2, 0, 1), trace_len)
    dq, dk, dv, db = pl.pallas_call(
        hand_out,
        out_shape=(
            jax.ShapeDtypeStruct((2 * BLOCK, 4096), BF),
            jax.ShapeDtypeStruct((2 * BLOCK, 512), BF),
            jax.ShapeDtypeStruct((2 * BLOCK, 512), BF),
            jax.ShapeDtypeStruct((32, 128), F32),
        ),
        in_specs=[vmem] * 4,
        out_specs=(any_,) * 4,
        scratch_shapes=[dma((4,))],
        compiler_params=pltpu.CompilerParams(has_side_effects=True),
        name="hand_out",
    )(*(pltpu.with_memory_space_constraint(a, pltpu.VMEM) for a in (dq, dk, dv, db)))
    return dq[None], dk[None], dv[None], db.reshape(4096)


def solution(mesh):
    return jax.shard_map(
        body,
        mesh=mesh,
        in_specs=(
            P("dp", "ctx", None),
            P("dp", "ctx", None),
            P("dp", "ctx", None),
            P("dp", "ctx", None),
            P(),
            P("dp", None, None),
            P("dp"),
        ),
        out_specs=(P("dp", "ctx", None), P("dp", "ctx", None), P("dp", "ctx", None), P()),
        check_vma=False,
    )
```

```python
import math

import jax
import jax.numpy as jnp
from jax import lax
from jax.experimental import pallas as pl
from jax.experimental.pallas import tpu as pltpu
from jax.sharding import PartitionSpec as P

HEAD_SIZE = 128
BLOCK = 128
PROMPT = 2
WINDOW = 3
NBLK = 128
N_CTX = 64
CHIPS = 32
NZ, NX, NY = 8, 4, 4
GROUPS = 2
PER_GROUP = 8
PIECE = BLOCK // NZ
SLOTS = PROMPT + WINDOW + 1
NEAR = 5
ROWS = 65536
SCALE = HEAD_SIZE ** (-0.5)
SCALE2 = SCALE * math.log2(math.e)
FAR = -1e30
BF, F32 = jnp.bfloat16, jnp.float32
MESH = pl.DeviceIdType.MESH


def dot(a, b, ca, cb):
    return lax.dot_general(a, b, (((ca,), (cb,)), ((), ())), preferred_element_type=F32)


def kernel(q_hbm, k_hbm, v_hbm, go_hbm, bias_ref, kb_ref, tl_ref,
           dq_ref, dk_ref, dv_ref, db_ref,
           qv, gv, stage, prompt, cand, acc, pacc, dqs, ret_s, ret_r, refl_r, sib_s, sib_r,
           ps, st1, st2s, st2, st3s, st3, bsrc, b1, b2s, b2, b3s, b3,
           q_sem, g_sem, kv_sem, own_sem, qx_ss, qx_rs, gx_ss, gx_rs, cx_ss, cx_rs,
           win_ss, win_rs, s1_ss, s1_rs, s2_ss, s2_rs, s3_ss, s3_rs, dq_ss, dq_rs,
           ret_ss, ret_rs, refl_rs, sib_ss, sib_rs, st1_ss, st1_rs, st2_ss, st2_rs, st3_ss, st3_rs,
           b1_ss, b1_rs, b2_ss, b2_rs, b3_ss, b3_rs):
    c = lax.axis_index("ctx")
    y = lax.axis_index("dp")
    core = lax.rem(c, 2)
    other = 1 - core
    chip = c // 2
    x = lax.rem(chip, NX)
    z = chip // NX
    sibling = chip * 2 + other
    is_root = c < PROMPT

    def at(zz, xx, rr):
        return (zz * NX + xx) * 2 + rr

    def rcopy(src, dst, ss, rs, dev):
        return pltpu.make_async_remote_copy(src_ref=src, dst_ref=dst, send_sem=ss, recv_sem=rs,
                                            device_id={"ctx": dev}, device_id_type=MESH)

    def wait_bytes(ref, sem):
        pltpu.make_async_copy(ref, ref, sem).wait()

    def loop(lo, hi, f):
        def step(i, carry):
            f(i)
            return carry
        lax.fori_loop(lo, hi, step, 0)

    def each(lo, hi, f):
        for i in range(lo, hi):
            f(i)

    def span(start, size):
        return pl.ds(pl.multiple_of(start, size), size)

    def kv_copy(half, kv, head, dst, sem):
        src = k_hbm if kv == 0 else v_hbm
        return pltpu.make_async_copy(src.at[half * BLOCK:(half + 1) * BLOCK, span(head * 128, 128)], dst, sem)

    def mine(half):
        return other if half == 0 else core

    def kv_stage(half, kv, head):
        return kv_copy(half, kv, head, stage.at[half, head, kv], kv_sem.at[half, kv, head])

    def kv_own(half, kv, g):
        return kv_copy(half, kv, core * 2 + g, cand.at[half, g, mine(half), kv], own_sem.at[half, kv, g])

    def q_own(src, dst, sem, g):
        return pltpu.make_async_copy(src.at[:, span(core * 2048 + g * 1024, 1024)], dst.at[1, g], sem.at[g])

    def q_cross(src, dst, ss, rs, g):
        return rcopy(src.at[:, span(other * 2048 + g * 1024, 1024)], dst.at[0, g], ss.at[g], rs.at[g], sibling)

    def start_stage(h):
        for half in range(2):
            for kv in range(2):
                kv_stage(half, kv, h).start()

    def start_own(g):
        for half in range(2):
            for kv in range(2):
                kv_own(half, kv, g).start()
        q_own(q_hbm, qv, q_sem, g).start()
        q_own(go_hbm, gv, g_sem, g).start()

    def zero_landing(g):
        for half in range(2):
            ret_r[half, g] = jnp.zeros((2, 2, 2, BLOCK, 128), BF)
        refl_r[g] = jnp.zeros((2, 2, BLOCK, 128), BF)
    loop(0, GROUPS, zero_landing)

    barrier = pltpu.get_barrier_semaphore()

    def greet(dev, yy):
        pl.semaphore_signal(barrier, inc=1, device_id={"ctx": dev, "dp": yy}, device_id_type=MESH)

    def greet_near(k):
        away = lax.rem(chip + CHIPS - 2 + k, CHIPS)

        @pl.when(k != 2)
        def _():
            greet(away * 2, y)
            greet(away * 2 + 1, y)
    loop(0, 5, greet_near)

    gi = z * 2 + core

    def greet_group(k):
        j = lax.rem(gi + k, 16)
        greet(at(j // 2, x, lax.rem(j, 2)), y)
    loop(1, 16, greet_group)

    def greet_row(k):
        greet(at(z, lax.rem(x + k, NX), core), y)
    loop(1, NX, greet_row)

    def greet_y(k):
        yy = lax.rem(y + k, NY)
        greet(c, yy)
        greet(sibling, yy)
    loop(1, NY, greet_y)

    loop(0, 4, start_stage)
    loop(0, GROUPS, start_own)

    def zero(g):
        for half in range(2):
            acc[half, g] = jnp.zeros((NEAR, 2, BLOCK, 128), F32)
        pacc[g] = jnp.zeros((PROMPT, 2, BLOCK, 128), F32)
        bsrc[g] = jnp.zeros((8, 128), F32)
    loop(0, GROUPS, zero)

    def wait_stage(h):
        for half in range(2):
            for kv in range(2):
                kv_stage(half, kv, h).wait()
    loop(0, 4, wait_stage)

    pl.semaphore_wait(barrier, 8 + 15 + 3 + 6)

    def rows16(p):
        return span(p * PIECE, PIECE)

    def scatter_prompt(g):
        @pl.when(is_root)
        def _():
            prompt[g, c, :, 0:PIECE, :] = stage[0, c * 2 + g, :, 0:PIECE, :]

            def scatter(k):
                j = lax.rem(c + k, 16)
                p, r = j // 2, lax.rem(j, 2)
                rcopy(stage.at[0, r * 2 + g, :, rows16(p), :], prompt.at[g, c, :, rows16(p), :],
                      s1_ss.at[g], s1_rs.at[g, c], at(p, 0, r)).start()
            loop(1, 16, scatter)
    scatter_prompt(0)

    def win_low(g, r, far):
        dst = lax.rem(chip + 1 + far, CHIPS) * 2 + r
        slot = 4 if far else 1 + 2 - core
        return rcopy(stage.at[0, r * 2 + g], cand.at[0, g, slot], win_ss.at[0, g, r, far], win_rs.at[0, g, slot - 2], dst)

    def win_up(g, r, far):
        dst = (chip - 1 - far) * 2 + r
        slot = 4 if far else 1 + 1 + core
        return rcopy(stage.at[1, r * 2 + g], cand.at[1, g, slot], win_ss.at[1, g, r, far], win_rs.at[1, g, slot - 2], dst)

    def win_fold(g, r):
        return rcopy(stage.at[0, r * 2 + g], cand.at[1, g, 4], win_ss.at[1, g, r, 1], win_rs.at[1, g, 2],
                     N_CTX - 4 + r)

    def cross(half, g):
        slot = mine(half)
        return rcopy(stage.at[half, other * 2 + g], cand.at[half, g, slot], cx_ss.at[half, g], cx_rs.at[half, g], sibling)

    def each_window(g, act):
        for r in range(2):
            act(win_low(g, r, 0))

            @pl.when(chip >= 1)
            def _():
                act(win_up(g, r, 0))

            @pl.when(core == 1)
            def _():
                act(win_low(g, r, 1))

            @pl.when((core == 0) & (chip >= 2))
            def _():
                act(win_up(g, r, 1))

            @pl.when(c == N_CTX - 1)
            def _():
                act(win_fold(g, r))
        for half in range(2):
            act(cross(half, g))
        act(q_cross(q_hbm, qv, qx_ss, qx_rs, g))
        act(q_cross(go_hbm, gv, gx_ss, gx_rs, g))

    def wait_near(g, half):
        cross(half, g).wait_recv()
        for slot in range(2, NEAR):
            rcopy(cand.at[half, g, slot], cand.at[half, g, slot], win_ss.at[0, g, 0, 0], win_rs.at[half, g, slot - 2],
                  sibling).wait_recv()

    def prompt_piece(g):
        return prompt.at[g, :, :, rows16(z), :]

    def prompt_row(g):
        @pl.when(x == 0)
        def _():
            for r in range(PROMPT):
                @pl.when(c != r)
                def _():
                    wait_bytes(prompt.at[g, r, :, rows16(z), :], s1_rs.at[g, r])

            def send(k):
                rcopy(prompt_piece(g), prompt_piece(g), s2_ss.at[g], s2_rs.at[g], at(z, k, core)).start()
            each(1, NX, send)

    def prompt_column(g):
        @pl.when(x > 0)
        def _():
            wait_bytes(prompt_piece(g), s2_rs.at[g])

        def send(k):
            rcopy(prompt_piece(g), prompt_piece(g), s3_ss.at[g], s3_rs.at[g], at(lax.rem(z + k, NZ), x, core)).start()
        each(1, NZ, send)

    def pieces(ref, g, n):
        return ref.at[g, :, :, pl.ds(0, n * PIECE), :]

    each_window(0, lambda copy: copy.start())
    prompt_row(0)
    prompt_column(0)

    width = PER_GROUP * 128
    kk = lax.broadcasted_iota(jnp.int32, (BLOCK, width), 0)
    qi = lax.rem(lax.broadcasted_iota(jnp.int32, (BLOCK, width), 1), BLOCK)
    lane = lax.rem(lax.broadcasted_iota(jnp.int32, (1, width), 1), BLOCK)
    length = tl_ref[0]

    def unit(g, half, role, leave=None):
        rho = core if role else other
        dev = chip * 2 + rho
        blk = jnp.where(half == 0, dev, NBLK - 1 - dev)
        base = jnp.where(half == 0, 1 - rho, rho)
        rows = span(half * BLOCK, BLOCK)
        bias = bias_ref[span(core * 16 + g * 8, 8), :]
        Q = jnp.concatenate(
            [(qv[role, g, rows, j * 128:(j + 1) * 128].astype(F32) + bias[j:j + 1]).astype(BF)
             for j in range(PER_GROUP)], 0)
        G = jnp.concatenate([gv[role, g, rows, j * 128:(j + 1) * 128] for j in range(PER_GROUP)], 0)
        K, V = (jnp.concatenate(
            [prompt[g, s, kv] for s in range(PROMPT)] + [cand[half, g, base + d, kv] for d in range(WINDOW + 1)], 0)
            for kv in range(2))
        off = [jnp.where(kb_ref[s, 0, blk] >= 0, 0.0, FAR).astype(F32) for s in range(SLOTS)]
        S = dot(K, Q, 1, 1)
        parts, m = [], None
        for s in range(SLOTS):
            v = S[s * 128:(s + 1) * 128]
            if s == PROMPT:
                v = jnp.where(kk <= qi, v, FAR)
            parts.append(v)
            mm = jnp.max(v, 0, keepdims=True) + off[s]
            m = mm if m is None else jnp.maximum(m, mm)
        m = m * SCALE2
        exps, tot = [], None
        for s in range(SLOTS):
            p = jnp.exp2(parts[s] * SCALE2 - (m - off[s]))
            exps.append(p)
            t = jnp.sum(p, 0, keepdims=True)
            tot = t if tot is None else tot + t
        inv = jnp.where(blk * BLOCK + lane < length, 1.0 / tot, 0.0)
        probs = jnp.concatenate(exps, 0) * inv
        low = probs.astype(BF)
        dP = dot(V, G, 1, 1)
        r = jnp.sum(probs * dP, 0, keepdims=True)
        dS = (probs * (dP - r)).astype(BF)
        dv = dot(low, G, 1, 0)
        dk = dot(dS, Q, 1, 0) * SCALE
        for kv, val in ((0, dk), (1, dv)):
            for s in range(PROMPT):
                pacc[g, s, kv] = pacc[g, s, kv] + val[s * 128:(s + 1) * 128]
            for d in range(WINDOW + 1):
                acc[half, g, base + d, kv] = acc[half, g, base + d, kv] + val[256 + d * 128:384 + d * 128]
        if leave is not None:
            leave()
        dq = dot(dS, K, 0, 0)
        for j in range(PER_GROUP):
            t = dq[j * 128:(j + 1) * 128] * SCALE
            if role:
                dq_ref[rows, span(core * 2048 + g * 1024 + j * 128, 128)] = t.astype(BF)
            else:
                dqs[g, rows, j * 128:(j + 1) * 128] = t.astype(BF)
            bsrc[g, j:j + 1, :] = bsrc[g, j:j + 1, :] + jnp.sum(t, 0, keepdims=True)

    def dq_cross(g, half):
        rows = span(half * BLOCK, BLOCK)
        return rcopy(dqs.at[g, rows, :], dq_ref.at[rows, span(core * 2048 + g * 1024, 1024)],
                     dq_ss.at[g, half], dq_rs.at[g, half], sibling)

    def ret_low(g, e):
        far = 1 if e == 3 else 0
        return rcopy(ret_s.at[0, g, e - 1], ret_r.at[0, g, core, far], ret_ss.at[0, g, e - 1],
                     ret_rs.at[0, g, core, far], lax.rem(chip * 2 + N_CTX - e, N_CTX))

    def ret_up(g, e):
        far = 1 if e == 3 else 0
        return rcopy(ret_s.at[1, g, e - 1], ret_r.at[1, g, core, far], ret_ss.at[1, g, e - 1],
                     ret_rs.at[1, g, core, far], chip * 2 + 1 + e)

    def ret_fold(g):
        return rcopy(ret_s.at[1, g, 2], refl_r.at[g, core], ret_ss.at[1, g, 2], refl_rs.at[g, core], N_CTX - 1)

    def sib_copy(g, half):
        return rcopy(sib_s.at[half, g], sib_r.at[half, g], sib_ss.at[half, g], sib_rs.at[half, g], sibling)

    def each_low(g, act):
        for e in range(1, WINDOW + 1):
            act(ret_low(g, e))
        act(sib_copy(g, 0))

    def each_up(g, act):
        for e in range(1, WINDOW + 1):
            @pl.when(chip * 2 + 1 + e < N_CTX)
            def _():
                act(ret_up(g, e))

        @pl.when(chip == CHIPS - 2)
        def _():
            act(ret_fold(g))
        act(sib_copy(g, 1))

    def send_low(g):
        for e in range(WINDOW):
            ret_s[0, g, e] = acc[0, g, 2 + e].astype(BF)
        sib_s[0, g] = acc[0, g, core].astype(BF)
        each_low(g, lambda copy: copy.start())

    def send_up(g):
        for e in range(WINDOW):
            ret_s[1, g, e] = acc[1, g, 2 + e].astype(BF)
        sib_s[1, g] = acc[1, g, other].astype(BF)
        each_up(g, lambda copy: copy.start())

    def fold_sums(g):
        for e in range(WINDOW):
            acc[0, g, e] = acc[0, g, e] + acc[1, g, 2 + e]

    def wait_recv(ref, sem):
        rcopy(ref, ref, win_ss.at[0, 0, 0, 0], sem, sibling).wait_recv()

    def wait_ret(g):
        for r in range(2):
            wait_recv(ret_r.at[0, g, r, 0], ret_rs.at[0, g, r, 0])

            @pl.when(core == 1)
            def _():
                wait_recv(ret_r.at[0, g, r, 1], ret_rs.at[0, g, r, 1])

            @pl.when(chip >= 1)
            def _():
                wait_recv(ret_r.at[1, g, r, 0], ret_rs.at[1, g, r, 0])

            @pl.when((core == 0) & (chip >= 2))
            def _():
                wait_recv(ret_r.at[1, g, r, 1], ret_rs.at[1, g, r, 1])

            @pl.when(c == N_CTX - 1)
            def _():
                wait_recv(refl_r.at[g, r], refl_rs.at[g, r])
        for half in range(2):
            wait_recv(sib_r.at[half, g], sib_rs.at[half, g])

    def send_shared(g):
        ps[g] = pacc[g].astype(BF)

        def send(k):
            zj = lax.rem(z + k, NZ)
            dev = at(zj, x, core)
            rcopy(ps.at[g, :, :, rows16(zj), :], st1.at[g, z], st1_ss.at[g], st1_rs.at[g], dev).start()
        each(1, NZ, send)
        st1[g, z] = ps[g, :, :, rows16(z), :]

    def total_of(ref, g, n):
        total = ref[g, 0].astype(F32)
        for k in range(1, n):
            total = total + ref[g, k].astype(F32)
        return total

    def step1(g):
        wait_bytes(st1.at[g, pl.ds(0, NZ - 1)], st1_rs.at[g])
        st2s[g] = total_of(st1, g, NZ).astype(BF)

        @pl.when(x == 0)
        def _():
            st2[g, 0] = st2s[g]

        @pl.when(x > 0)
        def _():
            rcopy(st2s.at[g], st2.at[g, x], st2_ss.at[g], st2_rs.at[g], at(z, 0, core)).start()
    def to_root(g, root):
        return rcopy(st3s.at[g, root], st3.at[g, core * NZ + z], st3_ss.at[g, root], st3_rs.at[g], root)

    def step2(g):
        @pl.when(x == 0)
        def _():
            wait_bytes(st2.at[g, pl.ds(0, NX - 1)], st2_rs.at[g])
            st3s[g] = total_of(st2, g, NX).astype(BF)
            for root in range(PROMPT):
                @pl.when(c == root)
                def _():
                    st3[g, root * NZ] = st3s[g, root]

                @pl.when(c != root)
                def _():
                    to_root(g, root).start()
    def send_bias():
        def send(k):
            rcopy(bsrc, b1.at[z], b1_ss, b1_rs, at(lax.rem(z + k, NZ), x, core)).start()
        each(1, NZ, send)
        b1[z] = bsrc[...]

    def sum_bias(ref, n):
        total = ref[0]
        for k in range(1, n):
            total = total + ref[k]
        return total

    def bias1():
        wait_bytes(b1.at[pl.ds(0, NZ - 1)], b1_rs)
        total = sum_bias(b1, NZ)
        b2s[...] = total
        b2[x] = total

        def send(k):
            rcopy(b2s, b2.at[x], b2_ss, b2_rs, at(z, lax.rem(x + k, NX), core)).start()
        each(1, NX, send)

    def bias2():
        wait_bytes(b2.at[pl.ds(0, NX - 1)], b2_rs)
        total = sum_bias(b2, NX)
        b3s[...] = total
        b3[core * NY + y] = total

        def send(k):
            j = lax.rem(core * NY + y + k, 2 * NY)
            pltpu.make_async_remote_copy(
                src_ref=b3s, dst_ref=b3.at[core * NY + y], send_sem=b3_ss, recv_sem=b3_rs,
                device_id={"ctx": chip * 2 + j // NY, "dp": lax.rem(j, NY)}, device_id_type=MESH).start()
        each(1, 2 * NY, send)

    def bias3():
        wait_bytes(b3.at[pl.ds(0, 2 * NY - 1)], b3_rs)
        for r in range(2):
            total = b3[r * NY]
            for k in range(1, NY):
                total = total + b3[r * NY + k]
            for g in range(GROUPS):
                db_ref[r * 16 + g * 8:r * 16 + g * 8 + 8, :] = total[g] * (1.0 / math.sqrt(ROWS))

    def finish(g):
        wait_ret(g)
        for t in range(2):
            r = other if t else core
            cols = span((r * 2 + g) * 128, 128)
            for half in range(2):
                for kv, out in ((0, dk_ref), (1, dv_ref)):
                    total = sib_r[half, g, kv].astype(F32) if t else acc[half, g, mine(half), kv]
                    for far in range(2):
                        total = total + ret_r[half, g, r, far, kv].astype(F32)
                    if half == 0:
                        total = total + refl_r[g, r, kv].astype(F32)

                        @pl.when(is_root)
                        def _():
                            pacc[g, t, kv] = total
                    out[half * BLOCK:(half + 1) * BLOCK, cols] = total.astype(BF)

    def finish_root(g):
        wait_bytes(st3.at[g, pl.ds(0, 2 * NZ - 1)], st3_rs.at[g])
        for t in range(2):
            r = other if t else core
            cols = span((r * 2 + g) * 128, 128)
            for kv, out in ((0, dk_ref), (1, dv_ref)):
                for p in range(NZ):
                    rr = slice(p * PIECE, (p + 1) * PIECE)
                    out[rr, cols] = (pacc[g, t, kv, rr, :] + st3[g, r * NZ + p, kv].astype(F32)).astype(BF)

    def main(i):
        g, half = i // 2, lax.rem(i, 2)

        @pl.when(half == 0)
        def _():
            for kv in range(2):
                kv_own(0, kv, g).wait()
                kv_own(1, kv, g).wait()
            q_own(q_hbm, qv, q_sem, g).wait()
            q_own(go_hbm, gv, g_sem, g).wait()
            q_cross(q_hbm, qv, qx_ss, qx_rs, g).wait_recv()
            q_cross(go_hbm, gv, gx_ss, gx_rs, g).wait_recv()
            wait_near(g, 0)
            wait_bytes(pieces(prompt, g, NZ - 1), s3_rs.at[g])

        @pl.when(i == 0)
        def _():
            scatter_prompt(1)
            each_window(1, lambda copy: copy.start())

        @pl.when(half == 1)
        def _():
            cross(1, g).wait_recv()

            @pl.when(chip < CHIPS - 1)
            def _():
                for slot in range(2, NEAR):
                    wait_recv(cand.at[1, g, slot], win_rs.at[1, g, slot - 2])

            @pl.when(chip == CHIPS - 1)
            def _():
                for slot in range(2, NEAR):
                    cand[1, g, slot] = cand[0, g, slot - 2]
        unit(g, half, 0)
        dq_cross(g, half).start()

        @pl.when(i == 0)
        def _():
            prompt_row(1)

        @pl.when(i == 2)
        def _():
            step1(0)

        def leave():
            @pl.when(half == 1)
            def _():
                send_shared(g)

                @pl.when(chip == CHIPS - 1)
                def _():
                    fold_sums(g)
                    send_low(g)
                send_up(g)

            @pl.when((half == 0) & (chip < CHIPS - 1))
            def _():
                send_low(g)
        unit(g, half, 1, leave)

        @pl.when(i == 0)
        def _():
            prompt_column(1)

        @pl.when(i == 2)
        def _():
            step2(0)
    loop(0, 2 * GROUPS, main)

    def drain(g):
        for half in range(2):
            dq_cross(g, half).wait()
        each_window(g, lambda copy: copy.wait_send())
        each_low(g, lambda copy: copy.wait_send())
        each_up(g, lambda copy: copy.wait_send())

        @pl.when(is_root)
        def _():
            wait_bytes(st3.at[g, pl.ds(0, 2 * NZ - 1)], s1_ss.at[g])

        @pl.when(x == 0)
        def _():
            wait_bytes(pieces(prompt, g, NX - 1), s2_ss.at[g])
            for root in range(PROMPT):
                @pl.when(c != root)
                def _():
                    to_root(g, root).wait_send()

        @pl.when(x > 0)
        def _():
            wait_bytes(st2s.at[g], st2_ss.at[g])
        wait_bytes(pieces(prompt, g, NZ - 1), s3_ss.at[g])
        wait_bytes(st1.at[g, pl.ds(0, NZ - 1)], st1_ss.at[g])

    send_bias()
    finish(0)

    @pl.when(is_root)
    def _():
        finish_root(0)
    step1(1)
    bias1()
    drain(0)
    step2(1)
    bias2()
    finish(1)
    drain(1)
    wait_bytes(b1.at[pl.ds(0, NZ - 1)], b1_ss)
    wait_bytes(b2.at[pl.ds(0, NX - 1)], b2_ss)

    @pl.when(is_root)
    def _():
        finish_root(1)
    bias3()
    wait_bytes(b3.at[pl.ds(0, 2 * NY - 1)], b3_ss)


def hand_out(dq, dk, dv, db, dq_out, dk_out, dv_out, db_out, sems):
    copies = [pltpu.make_async_copy(a, b, sems.at[i])
              for i, (a, b) in enumerate(((dq, dq_out), (dk, dk_out), (dv, dv_out), (db, db_out)))]
    for copy in copies:
        copy.start()
    for copy in copies:
        copy.wait()


def body(query_in, key_in, value_rows_input, grad_out, query_bias, key_blocks, trace_len):
    any_ = pl.BlockSpec(memory_space=pl.ANY)
    vmem = pl.BlockSpec(memory_space=pltpu.VMEM)
    smem = pl.BlockSpec(memory_space=pltpu.SMEM)
    dma = pltpu.SemaphoreType.DMA
    tile = (2, BLOCK, 128)
    G = GROUPS

    def many(*dims):
        return pltpu.VMEM(dims + tile, BF)
    part = (PROMPT, 2, PIECE, 128)
    dq, dk, dv, db = pl.pallas_call(
        kernel,
        out_shape=(
            pltpu.VMEM((2 * BLOCK, 4096), BF),
            pltpu.VMEM((2 * BLOCK, 512), BF),
            pltpu.VMEM((2 * BLOCK, 512), BF),
            pltpu.VMEM((32, 128), F32),
        ),
        in_specs=[any_, any_, any_, any_, vmem, smem, smem],
        out_specs=(vmem, vmem, vmem, vmem),
        scratch_shapes=[
            pltpu.VMEM((2, G, 2 * BLOCK, 1024), BF), pltpu.VMEM((2, G, 2 * BLOCK, 1024), BF),
            many(2, 4), many(G, PROMPT), many(2, G, NEAR),
            pltpu.VMEM((2, G, NEAR) + tile, F32), pltpu.VMEM((G, PROMPT) + tile, F32),
            pltpu.VMEM((G, 2 * BLOCK, 1024), BF),
            many(2, G, WINDOW), many(2, G, 2, 2), many(G, 2), many(2, G), many(2, G),
            many(G, PROMPT),
            pltpu.VMEM((G, NZ) + part, BF), pltpu.VMEM((G,) + part, BF), pltpu.VMEM((G, NX) + part, BF),
            pltpu.VMEM((G,) + part, BF), pltpu.VMEM((G, 2 * NZ, 2, PIECE, 128), BF),
            pltpu.VMEM((G, 8, 128), F32), pltpu.VMEM((NZ, G, 8, 128), F32),
            pltpu.VMEM((G, 8, 128), F32), pltpu.VMEM((NX, G, 8, 128), F32),
            pltpu.VMEM((G, 8, 128), F32), pltpu.VMEM((2 * NY, G, 8, 128), F32),
            dma((G,)), dma((G,)), dma((2, 2, 4)), dma((2, 2, G)),
            dma((G,)), dma((G,)), dma((G,)), dma((G,)), dma((2, G)), dma((2, G)),
            dma((2, G, 2, 2)), dma((2, G, WINDOW)),
            dma((G,)), dma((G, PROMPT)), dma((G,)), dma((G,)), dma((G,)), dma((G,)), dma((G, 2)), dma((G, 2)),
            dma((2, G, WINDOW)), dma((2, G, 2, 2)), dma((G, 2)), dma((2, G)), dma((2, G)),
            dma((G,)), dma((G,)), dma((G,)), dma((G,)), dma((G, PROMPT)), dma((G,)),
            dma, dma, dma, dma, dma, dma,
        ],
        compiler_params=pltpu.CompilerParams(
            collective_id=0, has_side_effects=True, vmem_limit_bytes=58 * 2**20),
        name="attention",
    )(query_in[0], key_in[0], value_rows_input[0], grad_out[0], query_bias.reshape(32, 128),
      key_blocks.transpose(2, 0, 1), trace_len)
    dq, dk, dv, db = pl.pallas_call(
        hand_out,
        out_shape=(
            jax.ShapeDtypeStruct((2 * BLOCK, 4096), BF),
            jax.ShapeDtypeStruct((2 * BLOCK, 512), BF),
            jax.ShapeDtypeStruct((2 * BLOCK, 512), BF),
            jax.ShapeDtypeStruct((32, 128), F32),
        ),
        in_specs=[vmem] * 4,
        out_specs=(any_,) * 4,
        scratch_shapes=[dma((4,))],
        compiler_params=pltpu.CompilerParams(has_side_effects=True),
        name="hand_out",
    )(*(pltpu.with_memory_space_constraint(a, pltpu.VMEM) for a in (dq, dk, dv, db)))
    return dq[None], dk[None], dv[None], db.reshape(4096)


def solution(mesh):
    return jax.shard_map(
        body,
        mesh=mesh,
        in_specs=(
            P("dp", "ctx", None),
            P("dp", "ctx", None),
            P("dp", "ctx", None),
            P("dp", "ctx", None),
            P(),
            P("dp", None, None),
            P("dp"),
        ),
        out_specs=(P("dp", "ctx", None), P("dp", "ctx", None), P("dp", "ctx", None), P()),
        check_vma=False,
    )
```
